32 devices in a mesh: groups: 2 (over x), slab: 16 (over z, y, core).
Axes of the slice: x: 2, y: 2, z: 4, core: 2. Of those that a mesh axis runs over, the one named last changes fastest.
Arguments:
- latent: bfloat16 [64, 32, 2048], P(None, ('groups', 'slab')), parts along dimension 1, may hold values from -6 to 6
- conv1_weight: bfloat16 [27, 64, 64], replicated, may hold values from -0.15625 to 0.15625
- conv2_weight: bfloat16 [27, 64, 64], replicated, may hold values from -0.15625 to 0.15625
- head: bfloat16 [64], replicated, may hold values from -2 to 2
- p_prev: float32 [32, 16, 64, 128], P(('groups', 'slab')), parts along dimension 0, may hold values from -6 to 6
- p_cur: float32 [32, 16, 64, 128], P(('groups', 'slab')), parts along dimension 0, may hold values from -6 to 6
- adjoint: bfloat16 [4, 32, 16, 64, 128], P(None, ('groups', 'slab')), parts along dimension 1, may hold values from -6 to 6
- wavelet: float32 [16, 4], P('groups'), parts along dimension 0, may hold values from -12 to 12
- sources: int32 [16, 3], P('groups'), parts along dimension 0, may hold values from 0 to 127, as said below
- receivers: int32 [16, 3, 128], P('groups'), parts along dimension 0, may hold values from 0 to 127, as said below
Outputs:
- pressure_final: float32 [32, 16, 64, 128], P(('groups', 'slab')), parts along dimension 0
- traces: float32 [16, 4, 128], P('groups'), parts along dimension 0
- gradient: float32 [32, 2048], P(('groups', 'slab')), parts along dimension 0
The draws below stay inside these ranges and needn't reach their ends.
There are 2 independent parts, one for each index of `groups`. The reference program is written for one: setup_inputs(seed, part) draws one part's arguments, and reference() takes and returns one part's arrays. A program takes and returns all parts, laid end to end along the dimension named above; an argument that names none is the same for every part. Nothing has to cross between parts.
Inputs may be any that keep to these rules, and one draw needn't show every extreme that they name: sources[s] is the source cell (depth, row, column) of shot s on the fine grid: depth below 32, row below 64, column below 128. receivers[s, :, k] is the cell (depth, row, column) of receiver k of shot s on the fine grid: depth below 32, row below 64, column below 128.
All inputs are finite; a program needn't handle non-finite values.
Results may differ from the reference program's by a relative error of at most 0.006.
Values may be sent and summed in bfloat16 or wider, within the bound.
No kernel may reach another device: no remote copies, remote signals or barrier semaphores. Data moves between devices by JAX's collectives and lax.ppermute only.
A program may use at most 64 MiB of HBM per device.

```python
import jax
import jax.numpy as jnp
from jax import lax

CH = 64
CY = 32
CX = 64
SHOTS = 8
STEPS = 4
NREC = 128
SLABS = 2
NZC = 16
FZ = 32
FPS = 16
FY = 64
FX = 128
SLOTS = 16


def draw_sources(key, part):
    key_depth, key_row, key_col, key_pick = jax.random.split(jax.random.fold_in(key, 11), 4)
    depths = jax.random.randint(key_depth, (SHOTS,), 0, FZ)
    rows_drawn = jax.random.randint(key_row, (SHOTS,), 0, FY)
    cols_drawn = jax.random.randint(key_col, (SHOTS,), 0, FX)
    chosen = jax.random.randint(key_pick, (), 0, SHOTS)
    marked = jnp.arange(SHOTS) == chosen
    depths = jnp.where(marked, FZ - 1, depths)
    rows_drawn = jnp.where(marked, FY - 1, rows_drawn)
    cols_drawn = jnp.where(marked, FX - 1, cols_drawn)
    return jnp.stack([depths, rows_drawn, cols_drawn], axis=1).astype(jnp.int32)


def draw_receivers(key, part):
    key_depth, key_row, key_col, key_pick = jax.random.split(jax.random.fold_in(key, 23), 4)
    depths = jax.random.randint(key_depth, (SHOTS, NREC), 0, FZ)
    rows_drawn = jax.random.randint(key_row, (SHOTS, NREC), 0, FY)
    cols_drawn = jax.random.randint(key_col, (SHOTS, NREC), 0, FX)
    chosen = jax.random.randint(key_pick, (SHOTS, 1), 0, NREC)
    marked = jnp.arange(NREC)[None, :] == chosen
    depths = jnp.where(marked, FZ - 1, depths)
    rows_drawn = jnp.where(marked, FY - 1, rows_drawn)
    cols_drawn = jnp.where(marked, FX - 1, cols_drawn)
    return jnp.stack([depths, rows_drawn, cols_drawn], axis=1).astype(jnp.int32)


def block_levels(rng, shape, shards, smallest, top_value):
    def one(position, blocks):
        draws = jax.random.uniform(jax.random.fold_in(jax.random.fold_in(rng, 6), position), (blocks,), jnp.float32, smallest / len(shards), top_value / len(shards))
        return jnp.repeat(jnp.exp(draws), shape[position] // blocks).reshape((-1,) + (1,) * (len(shape) - position - 1))

    factor_of = one(*shards[0])
    for cut in shards[1:]:
        factor_of = factor_of * one(*cut)
    return factor_of


def scatter_about(rng, shape, width, bound, cuts=(), held_as=jnp.bfloat16):
    drawn = jax.random.normal(rng, shape, jnp.float32) * width
    if len(cuts) > 0:
        drawn = block_levels(rng, shape, cuts, -0.22, 0.18) * drawn
    return jnp.clip(drawn, min=-bound, max=bound).astype(held_as)


def setup_inputs(seed: int = 0, part: int = 0) -> dict:
    keys = jax.random.split(jax.random.key(seed), 11)
    own_keys = jax.random.split(jax.random.fold_in(keys[10], part), 11)
    latent = scatter_about(own_keys[0], (CH, NZC, CY * CX), 1.0, 6.0, ((1, 16),))
    conv1_weight = scatter_about(keys[1], (27, CH, CH), (27 * CH) ** -0.5, 0.15625)
    conv2_weight = scatter_about(keys[2], (27, CH, CH), (27 * CH) ** -0.5, 0.15625)
    head = scatter_about(keys[3], (CH,), (CH // 8) ** -0.5, 2.0)
    p_prev = scatter_about(own_keys[4], (SLOTS, FPS, FY, FX), 1.0, 6.0, ((0, 16),), jnp.float32)
    p_cur = scatter_about(own_keys[5], (SLOTS, FPS, FY, FX), 1.0, 6.0, ((0, 16),), jnp.float32)
    adjoint = scatter_about(own_keys[6], (STEPS, SLOTS, FPS, FY, FX), 1.0, 6.0, ((1, 16),))
    wavelet = scatter_about(own_keys[7], (SHOTS, STEPS), 3.0, 12.0, (), jnp.float32)
    sources = draw_sources(jax.random.fold_in(jax.random.fold_in(keys[10], part), 71), part)
    receivers = draw_receivers(jax.random.fold_in(jax.random.fold_in(keys[10], part), 71), part)
    return dict(latent=latent, conv1_weight=conv1_weight, conv2_weight=conv2_weight, head=head, p_prev=p_prev, p_cur=p_cur, adjoint=adjoint, wavelet=wavelet, sources=sources, receivers=receivers)


stencil_weights = (-205.0 / 72.0, 8.0 / 5.0, -1.0 / 5.0, 8.0 / 315.0, -1.0 / 560.0)
lowest_speed = 1.5
speed_range = 3.0
courant = 0.088
leak_slope = 0.2

def conv_layer(activation, weight):
    planes = activation.shape[1]
    cell_count = activation.shape[2]
    extended = jnp.pad(activation, ((0, 0), (1, 1), (CX + 1, CX + 1)))
    columns = jnp.arange(cell_count) % CX
    accumulated = jnp.zeros((weight.shape[1], planes, cell_count), jnp.float32)
    tap_index = 0
    for depth_off in range(3):
        for row_off in (-1, 0, 1):
            for col_off in (-1, 0, 1):
                begin_at = CX + 1 + row_off * CX + col_off
                piece = extended[:, depth_off:depth_off + planes, begin_at:begin_at + cell_count]
                column_valid = ((columns + col_off >= 0) & (columns + col_off < CX)).astype(jnp.float32)
                accumulated = accumulated + jnp.einsum('oi,izn->ozn', weight[tap_index], piece * column_valid, precision=lax.Precision.HIGHEST)
                tap_index += 1
    return accumulated

def double_axis(values, axis):
    length = values.shape[axis]
    lower_side = jnp.concatenate([lax.slice_in_dim(values, 0, 1, axis=axis), lax.slice_in_dim(values, 0, length - 1, axis=axis)], axis=axis)
    upper_side = jnp.concatenate([lax.slice_in_dim(values, 1, length, axis=axis), lax.slice_in_dim(values, length - 1, length, axis=axis)], axis=axis)
    even_part = 0.75 * values + 0.25 * lower_side
    odd_part = 0.75 * values + 0.25 * upper_side
    new_shape = list(values.shape)
    new_shape[axis] = 2 * length
    return jnp.stack([even_part, odd_part], axis=axis + 1).reshape(new_shape)

def upsample_whole(coarse):
    grid = coarse.reshape(coarse.shape[0], CY, CX)
    return double_axis(double_axis(double_axis(grid, 0), 1), 2)

def stencil(extended):
    depth_total = extended.shape[0] - 8
    row_total = extended.shape[1]
    col_total = extended.shape[2]
    padded = jnp.pad(extended, ((0, 0), (4, 4), (4, 4)))

    def window(depth_at, row_at, col_at):
        return padded[depth_at:depth_at + depth_total, row_at:row_at + row_total, col_at:col_at + col_total]
    accumulated = 3.0 * stencil_weights[0] * window(4, 4, 4)
    for reach in range(1, 5):
        near_sum = window(4 - reach, 4, 4) + window(4 + reach, 4, 4)
        near_sum = near_sum + window(4, 4 - reach, 4) + window(4, 4 + reach, 4)
        near_sum = near_sum + window(4, 4, 4 - reach) + window(4, 4, 4 + reach)
        accumulated = accumulated + stencil_weights[reach] * near_sum
    return accumulated

def propagate(prev_field, field, adjoint_shot, pulses, source, station, courant_sq):
    correlation = jnp.zeros(field.shape, jnp.float32)
    samples_list = []
    for step_index in range(STEPS):
        laplace_term = stencil(jnp.pad(field, ((4, 4), (0, 0), (0, 0))))
        correlation = correlation + adjoint_shot[step_index].astype(jnp.float32) * laplace_term
        advanced = 2.0 * field - prev_field + courant_sq * laplace_term
        advanced = advanced.at[source[0], source[1], source[2]].add(pulses[step_index])
        samples_list.append(advanced[station[0], station[1], station[2]])
        prev_field, field = (field, advanced)
    return (field, jnp.stack(samples_list), correlation)

def reference(latent, conv1_weight, conv2_weight, head, p_prev, p_cur, adjoint, wavelet, sources, receivers):
    hidden = jax.nn.leaky_relu(conv_layer(latent.astype(jnp.float32), conv1_weight.astype(jnp.float32)), leak_slope).astype(jnp.bfloat16)
    second = jax.nn.leaky_relu(conv_layer(hidden.astype(jnp.float32), conv2_weight.astype(jnp.float32)), leak_slope)
    logits = jnp.einsum('c,czn->zn', head.astype(jnp.float32), second, precision=lax.Precision.HIGHEST)
    speed = (lowest_speed + speed_range * jax.nn.sigmoid(logits)).astype(jnp.bfloat16)
    coarse_speed = speed.astype(jnp.float32)
    fine_speed = upsample_whole(coarse_speed)
    courant_sq = (courant * fine_speed) ** 2

    def to_shots(field):
        return field.reshape(SLABS, SHOTS, FPS, FY, FX).transpose(1, 0, 2, 3, 4).reshape(SHOTS, FZ, FY, FX)
    prev_shots = to_shots(p_prev)
    cur_shots = to_shots(p_cur)
    adjoint_shots = adjoint.reshape(STEPS, SLABS, SHOTS, FPS, FY, FX).transpose(2, 0, 1, 3, 4, 5).reshape(SHOTS, STEPS, FZ, FY, FX)

    def one_shot(carried, inputs):
        prev_field, field, adjoint_shot, pulses, source, station = inputs
        final_field, samples, correlation = propagate(prev_field, field, adjoint_shot, pulses, source, station, courant_sq)
        return (carried + correlation, (final_field, samples))
    start_sum = jnp.zeros((FZ, FY, FX), jnp.float32)
    summed, outputs = lax.scan(one_shot, start_sum, (prev_shots, cur_shots, adjoint_shots, wavelet, sources, receivers))
    final_fields, traces = outputs
    pressure_final = final_fields.reshape(SHOTS, SLABS, FPS, FY, FX).transpose(1, 0, 2, 3, 4).reshape(SLOTS, FPS, FY, FX)
    fine_gradient = 2.0 * courant * courant * fine_speed * summed
    unused, pullback = jax.vjp(upsample_whole, coarse_speed)
    gradient = pullback(fine_gradient)[0]
    return (pressure_final, traces, gradient)
```

```python
import functools

import jax
import jax.numpy as jnp
import numpy as np
from jax import lax
from jax.experimental import pallas as pl
from jax.experimental.pallas import tpu as pltpu
from jax.sharding import PartitionSpec as P

CH = 64
CY = 32
CX = 64
FY = 64
FX = 128
CELLS = CY * CX
SHOTS = 8
STEPS = 4
NREC = 128
PLANES = 16
REACH = 4
CUR_RIM = REACH * STEPS
PREV_RIM = CUR_RIM - REACH
RIM_PLANES = CUR_RIM + PREV_RIM
EXT = PLANES + 2 * CUR_RIM
PAD = 8
ROWS = FY + 2 * PAD

stencil_weights = (-205.0 / 72.0, 8.0 / 5.0, -1.0 / 5.0, 8.0 / 315.0, -1.0 / 560.0)
lowest_speed = 1.5
speed_range = 3.0
courant = 0.088
leak_slope = 0.2

VMEM = pl.BlockSpec(memory_space=pltpu.VMEM)
SMEM = pl.BlockSpec(memory_space=pltpu.SMEM)
PARAMS = pltpu.CompilerParams(vmem_limit_bytes=48 * 1024 * 1024)


def doubling_matrix(length):
    matrix = np.zeros((2 * length, length), np.float32)
    for k in range(length):
        matrix[2 * k, k] += 0.75
        matrix[2 * k, max(k - 1, 0)] += 0.25
        matrix[2 * k + 1, k] += 0.75
        matrix[2 * k + 1, min(k + 1, length - 1)] += 0.25
    return matrix


def plane_matrices():
    across = doubling_matrix(CX)
    down = doubling_matrix(CY)
    widen = np.zeros((128, 256), np.float32)
    widen[:64, :128] = across.T
    widen[64:, 128:] = across.T
    tall = np.concatenate([down[:, 0::2], down[:, 1::2]], axis=1)
    tall_twice = np.concatenate([tall, tall], axis=1)
    short_twice = np.concatenate([tall.T, tall.T], axis=1)
    narrow = widen.T
    return tuple(jnp.asarray(m, jnp.bfloat16) for m in (widen, tall_twice, short_twice, narrow))


def halves(value):
    high = value.astype(jnp.bfloat16)
    low = (value - high.astype(jnp.float32)).astype(jnp.bfloat16)
    return high, low


def leaky(value):
    return jnp.where(value > 0, value, leak_slope * value)


def conv(low_ref, mid_ref, high_ref, weight_ref, fields, packed):
    column = lax.broadcasted_iota(jnp.int32, (CH, CELLS), 1) % CX
    for depth, ref in enumerate((low_ref, mid_ref, high_ref)):
        plane = ref[...]
        wide = plane.astype(jnp.float32)
        left = jnp.where(column == 0, 0.0, pltpu.roll(wide, 1, 1)).astype(jnp.bfloat16)
        right = jnp.where(column == CX - 1, 0.0, pltpu.roll(wide, CELLS - 1, 1)).astype(jnp.bfloat16)
        for place, piece in enumerate((left, plane, right)):
            begin = (3 * depth + place) * CH
            fields[begin : begin + CH, :] = piece
    for depth in range(3):
        for row in range(3):
            for place in range(3):
                tap = 9 * depth + 3 * row + place
                begin = (3 * depth + place) * CH
                packed[row * CH : (row + 1) * CH, begin : begin + CH] = weight_ref[tap]
    products = jnp.dot(packed[...], fields[...], preferred_element_type=jnp.float32)
    cell = lax.broadcasted_iota(jnp.int32, (CH, CELLS), 1)
    above = jnp.where(cell < CX, 0.0, pltpu.roll(products[:CH], CX, 1))
    below = jnp.where(cell >= CELLS - CX, 0.0, pltpu.roll(products[2 * CH :], CELLS - CX, 1))
    return products[CH : 2 * CH] + above + below


def first_kernel(low_ref, mid_ref, high_ref, weight_ref, out_ref, fields, packed):
    out_ref[...] = leaky(conv(low_ref, mid_ref, high_ref, weight_ref, fields, packed)).astype(
        jnp.bfloat16
    )


def second_kernel(low_ref, mid_ref, high_ref, weight_ref, head_ref, out_ref, fields, packed):
    second = leaky(conv(low_ref, mid_ref, high_ref, weight_ref, fields, packed))
    logits = jnp.sum(second * head_ref[...], axis=0, keepdims=True)
    speed = lowest_speed + speed_range * jax.nn.sigmoid(logits)
    for j in range(16):
        out_ref[j : j + 1, :] = speed[:, 128 * j : 128 * (j + 1)].astype(jnp.bfloat16)


CONV_SCRATCH = [
    pltpu.VMEM((9 * CH, CELLS), jnp.bfloat16),
    pltpu.VMEM((3 * CH, 9 * CH), jnp.bfloat16),
]


def first_conv(low, mid, high, weight):
    return pl.pallas_call(
        first_kernel,
        out_shape=jax.ShapeDtypeStruct((CH, CELLS), jnp.bfloat16),
        in_specs=[VMEM] * 4,
        out_specs=VMEM,
        scratch_shapes=CONV_SCRATCH,
        compiler_params=PARAMS,
    )(low, mid, high, weight)


def second_conv(low, mid, high, weight, head):
    return pl.pallas_call(
        second_kernel,
        out_shape=jax.ShapeDtypeStruct((16, 128), jnp.bfloat16),
        in_specs=[VMEM] * 5,
        out_specs=VMEM,
        scratch_shapes=CONV_SCRATCH,
        compiler_params=PARAMS,
    )(low, mid, high, weight, head)


def laplace(field, plane, lane):
    middle = field[plane, PAD : PAD + FY, :]
    total = (3.0 * stencil_weights[0]) * middle
    for reach in range(1, REACH + 1):
        near = field[plane - reach, PAD : PAD + FY, :] + field[plane + reach, PAD : PAD + FY, :]
        near = near + field[plane, PAD - reach : PAD - reach + FY, :]
        near = near + field[plane, PAD + reach : PAD + reach + FY, :]
        near = near + jnp.where(lane < reach, 0.0, pltpu.roll(middle, reach, 1))
        near = near + jnp.where(lane >= FX - reach, 0.0, pltpu.roll(middle, FX - reach, 1))
        total = total + stencil_weights[reach] * near
    return total


def wave_kernel(
    info,
    pulses,
    stations,
    cur_ref,
    prev_ref,
    low_rim,
    high_rim,
    adjoint_ref,
    own_speed,
    low_speed,
    high_speed,
    pick_ref,
    widen_ref,
    tall_ref,
    short_ref,
    narrow_ref,
    final_ref,
    terms_ref,
    edges_ref,
    records_ref,
    field_a,
    field_b,
    factor,
    coarse,
    speed,
    total,
    rows,
):
    shot = info[0]
    has_low = info[1] == 1
    has_high = info[2] == 1
    lane = lax.broadcasted_iota(jnp.int32, (FY, FX), 1)

    def clear(plane, _):
        for field in (field_a, field_b):
            field[plane, :PAD, :] = jnp.zeros((PAD, FX), jnp.float32)
            field[plane, PAD + FY :, :] = jnp.zeros((PAD, FX), jnp.float32)
        return 0

    lax.fori_loop(0, EXT, clear, 0)
    inner = slice(PAD, PAD + FY)

    def load_own(plane, _):
        field_a[CUR_RIM + plane, inner, :] = cur_ref[plane]
        field_b[CUR_RIM + plane, inner, :] = prev_ref[plane]
        return 0

    lax.fori_loop(0, PLANES, load_own, 0)

    def load_rim(rim, at_cur, at_prev):
        def one(plane, _):
            field_a[at_cur + plane, inner, :] = rim[plane].astype(jnp.float32)
            return 0

        lax.fori_loop(0, CUR_RIM, one, 0)

        def two(plane, _):
            field_b[at_prev + plane, inner, :] = rim[CUR_RIM + plane].astype(jnp.float32)
            return 0

        lax.fori_loop(0, PREV_RIM, two, 0)

    def no_rim(at):
        def one(plane, _):
            for field in (field_a, field_b):
                field[at + plane, inner, :] = jnp.zeros((FY, FX), jnp.float32)
            return 0

        lax.fori_loop(0, REACH, one, 0)

    @pl.when(has_low)
    def _():
        load_rim(low_rim, 0, REACH)

    @pl.when(jnp.logical_not(has_low))
    def _():
        no_rim(CUR_RIM - REACH)

    @pl.when(has_high)
    def _():
        load_rim(high_rim, CUR_RIM + PLANES, CUR_RIM + PLANES)

    @pl.when(jnp.logical_not(has_high))
    def _():
        no_rim(CUR_RIM + PLANES)

    def widen_block(ref, at):
        block = ref[...].reshape(SHOTS * 16, 128)
        wide = jnp.dot(block, widen_ref[...], preferred_element_type=jnp.float32)
        for j in range(SHOTS):
            piece = wide[16 * j : 16 * (j + 1)]
            both = jnp.concatenate([piece[:, :128], piece[:, 128:]], axis=0)
            high, low = halves(both)
            stacked = jnp.concatenate([high, low], axis=0)
            coarse[at + (shot ^ j)] = jnp.dot(
                tall_ref[...], stacked, preferred_element_type=jnp.float32
            )

    widen_block(own_speed, SHOTS)

    @pl.when(has_low)
    def _():
        widen_block(low_speed, 0)

    @pl.when(jnp.logical_not(has_low))
    def _():
        coarse[SHOTS - 1] = coarse[SHOTS]

    @pl.when(has_high)
    def _():
        widen_block(high_speed, 2 * SHOTS)

    @pl.when(jnp.logical_not(has_high))
    def _():
        coarse[2 * SHOTS] = coarse[2 * SHOTS - 1]

    low_count = jnp.where(has_low, 1, 0)
    high_count = jnp.where(has_high, 1, 0)

    def refine(k, _):
        here = 0.75 * coarse[k]
        even = here + 0.25 * coarse[k - 1]
        odd = here + 0.25 * coarse[k + 1]
        speed[2 * k] = even
        speed[2 * k + 1] = odd
        factor[2 * k] = (courant * even) * (courant * even)
        factor[2 * k + 1] = (courant * odd) * (courant * odd)
        return 0

    lax.fori_loop(
        SHOTS - low_count * (PREV_RIM // 2),
        2 * SHOTS + high_count * (PREV_RIM // 2),
        refine,
        0,
    )

    source_plane = info[3] + CUR_RIM
    source_row = info[4] + PAD
    source_column = info[5]
    lane_row = lax.broadcasted_iota(jnp.int32, (1, FX), 1)

    for step in range(STEPS):
        now, other = (field_a, field_b) if step % 2 == 0 else (field_b, field_a)
        reach_out = CUR_RIM - REACH * (step + 1)

        def advance(plane, lap):
            other[plane, inner, :] = (
                2.0 * now[plane, inner, :] - other[plane, inner, :] + factor[plane] * lap
            )

        def rim_plane(plane, _):
            advance(plane, laplace(now, plane, lane))
            return 0

        def own_plane(plane, _):
            lap = laplace(now, plane + CUR_RIM, lane)
            term = adjoint_ref[step, plane].astype(jnp.float32) * lap
            if step == 0:
                total[plane] = term
            else:
                total[plane] = total[plane] + term
            advance(plane + CUR_RIM, lap)
            return 0

        first = CUR_RIM - low_count * reach_out
        last = CUR_RIM + PLANES + high_count * reach_out
        if reach_out > 0:
            lax.fori_loop(first, CUR_RIM, rim_plane, 0)
        lax.fori_loop(0, PLANES, own_plane, 0)
        if reach_out > 0:
            lax.fori_loop(CUR_RIM + PLANES, last, rim_plane, 0)

        @pl.when((source_plane >= first) & (source_plane < last))
        def _():
            cell = other[source_plane, pl.ds(source_row, 1), :]
            other[source_plane, pl.ds(source_row, 1), :] = cell + jnp.where(
                lane_row == source_column, pulses[step], 0.0
            )

        def collect(k, _):
            rows[pl.ds(k, 1), :] = other[stations[0, k], pl.ds(stations[1, k], 1), :]
            return 0

        lax.fori_loop(0, NREC, collect, 0, unroll=8)
        records_ref[step : step + 1, :] = jnp.sum(
            (rows[...] * pick_ref[...]).T, axis=0, keepdims=True
        )

    result = field_a if STEPS % 2 == 0 else field_b

    def store(plane, _):
        final_ref[plane] = result[CUR_RIM + plane, inner, :]
        return 0

    lax.fori_loop(0, PLANES, store, 0)

    def scale(plane, _):
        total[plane] = (2.0 * courant * courant) * speed[CUR_RIM + plane] * total[plane]
        return 0

    lax.fori_loop(0, PLANES, scale, 0)

    shrunk = []
    for k in range(-1, SHOTS + 1):
        value = 0.0
        for plane, weight in ((2 * k - 1, 0.25), (2 * k, 0.75), (2 * k + 1, 0.75), (2 * k + 2, 0.25)):
            if 0 <= plane < PLANES:
                value = value + weight * total[plane]
        high, low = halves(value)
        stacked = jnp.concatenate([high, low], axis=0)
        shrunk.append(jnp.dot(short_ref[...], stacked, preferred_element_type=jnp.float32))
    sides = [jnp.concatenate([z[:16], z[16:]], axis=1) for z in shrunk]
    high, low = halves(jnp.concatenate(sides, axis=0))
    narrow = narrow_ref[...]
    out = jnp.dot(high, narrow, preferred_element_type=jnp.float32) + jnp.dot(
        low, narrow, preferred_element_type=jnp.float32
    )
    below = out[:16]
    above = out[16 * (SHOTS + 1) :]
    for k in range(SHOTS):
        piece = out[16 * (k + 1) : 16 * (k + 2)]
        if k == 0:
            piece = piece + jnp.where(has_low, 0.0, below)
        if k == SHOTS - 1:
            piece = piece + jnp.where(has_high, 0.0, above)
        terms_ref[shot ^ k] = piece
    edges_ref[0] = jnp.where(has_low, below, 0.0)
    edges_ref[1] = jnp.where(has_high, above, 0.0)


def wave(*args):
    return pl.pallas_call(
        wave_kernel,
        out_shape=(
            jax.ShapeDtypeStruct((PLANES, FY, FX), jnp.float32),
            jax.ShapeDtypeStruct((SHOTS, 16, 128), jnp.float32),
            jax.ShapeDtypeStruct((2, 16, 128), jnp.float32),
            jax.ShapeDtypeStruct((STEPS, NREC), jnp.float32),
        ),
        in_specs=[SMEM] * 3 + [VMEM] * 13,
        out_specs=(VMEM,) * 4,
        scratch_shapes=[
            pltpu.VMEM((EXT, ROWS, FX), jnp.float32),
            pltpu.VMEM((EXT, ROWS, FX), jnp.float32),
            pltpu.VMEM((EXT, FY, FX), jnp.float32),
            pltpu.VMEM((3 * SHOTS, FY, FX), jnp.float32),
            pltpu.VMEM((EXT, FY, FX), jnp.float32),
            pltpu.VMEM((PLANES, FY, FX), jnp.float32),
            pltpu.VMEM((NREC, FX), jnp.float32),
        ],
        compiler_params=PARAMS,
    )(*args)


def finish_kernel(info, term_ref, records_ref, gradient_ref, traces_ref):
    shot = info[0]
    for j in range(16):
        gradient_ref[:, 128 * j : 128 * (j + 1)] = term_ref[j : j + 1, :]
    for j in range(SHOTS):
        traces_ref[shot ^ j] = records_ref[j]


def finish(info, term, records):
    return pl.pallas_call(
        finish_kernel,
        out_shape=(
            jax.ShapeDtypeStruct((1, CELLS), jnp.float32),
            jax.ShapeDtypeStruct((SHOTS, STEPS, NREC), jnp.float32),
        ),
        in_specs=[SMEM, VMEM, VMEM],
        out_specs=(VMEM, VMEM),
        compiler_params=PARAMS,
    )(info, term, records)


def shift(value, steps):
    count = lax.axis_size("slab")
    begin, end = max(0, -steps), min(count, count - steps)
    return lax.ppermute(value, "slab", [(source, source + steps) for source in range(begin, end)])


def partner(value, mask):
    count = lax.axis_size("slab")
    return lax.ppermute(value, "slab", [(source, source ^ mask) for source in range(count)])


def body(
    latent, conv1_weight, conv2_weight, head, p_prev, p_cur, adjoint, wavelet, sources, receivers
):
    position = lax.axis_index("slab")
    devices = lax.axis_size("slab")
    slabs = devices // SHOTS
    shot = position % SHOTS
    slab = position // SHOTS
    has_low = slab > 0
    has_high = slab < slabs - 1

    def exchange(to_low, to_high):
        if slabs == 2:
            got = partner(to_low if to_low is to_high else jnp.where(has_low, to_low, to_high), SHOTS)
            return got, got
        return shift(to_high, SHOTS), shift(to_low, -SHOTS)

    latent = latent.reshape(CH, CELLS)
    latent_low, latent_high = shift(latent, 1), shift(latent, -1)

    current = p_cur[0]
    previous = p_prev[0]
    rim_low, rim_high = exchange(
        jnp.concatenate([current, previous[:PREV_RIM]], axis=0).astype(jnp.bfloat16),
        jnp.concatenate([current, previous[PLANES - PREV_RIM :]], axis=0).astype(jnp.bfloat16),
    )

    hidden = first_conv(latent_low, latent, latent_high, conv1_weight)
    hidden_low, hidden_high = shift(hidden, 1), shift(hidden, -1)
    velocity = second_conv(
        hidden_low, hidden, hidden_high, conv2_weight, head.astype(jnp.float32)[:, None]
    )

    block = velocity[None]
    for bit in range(3):
        block = jnp.concatenate([block, partner(block, 1 << bit)], axis=0)
    speed_low, speed_high = exchange(block, block)

    source = lax.dynamic_index_in_dim(sources, shot, 0, keepdims=False)
    station = lax.dynamic_index_in_dim(receivers, shot, 0, keepdims=False)
    pulses = lax.dynamic_index_in_dim(wavelet, shot, 0, keepdims=False)
    offset = slab * PLANES
    info = jnp.stack(
        [
            shot,
            has_low.astype(jnp.int32),
            has_high.astype(jnp.int32),
            source[0] - offset,
            source[1],
            source[2],
        ]
    )
    depth = station[0] - offset
    inside = (depth >= 0) & (depth < PLANES)
    stations = jnp.stack([jnp.clip(depth, 0, PLANES - 1) + CUR_RIM, station[1] + PAD])
    pick = (
        (station[2][:, None] == jnp.arange(FX)[None, :]) & inside[:, None]
    ).astype(jnp.float32)
    final, terms, edges, record = wave(
        info,
        pulses,
        stations,
        current,
        previous,
        rim_low,
        rim_high,
        adjoint[:, 0],
        block,
        speed_low,
        speed_high,
        pick,
        *plane_matrices(),
    )

    if slabs == 2:
        message = jnp.concatenate([jnp.where(has_low, edges[0], edges[1]), record], axis=0)
        got = partner(message, SHOTS)
        edge_low = jnp.where(has_low, got[:16], 0.0)
        edge_high = jnp.where(has_high, got[:16], 0.0)
        record = record + got[16:]
    else:
        edge_low, edge_high = shift(edges[1], SHOTS), shift(edges[0], -SHOTS)
        mask = SHOTS
        while mask < devices:
            record = record + partner(record, mask)
            mask *= 2
    place = jnp.arange(SHOTS)[:, None, None]
    terms = terms + jnp.where(place == shot, edge_low, 0.0)
    terms = terms + jnp.where(place == shot ^ (SHOTS - 1), edge_high, 0.0)
    terms = terms.reshape(SHOTS * 16, 128)
    records = record
    for bit in reversed(range(3)):
        half = terms.shape[0] // 2
        size = records.shape[0]
        got = partner(jnp.concatenate([terms[half:], records], axis=0), 1 << bit)
        terms = terms[:half] + got[:half]
        records = jnp.concatenate([records, got[half:]], axis=0)
    order = [4 * (j & 1) + (j & 2) + (j >> 2) for j in range(SHOTS)]
    records = records.reshape(SHOTS, STEPS, NREC)
    records = jnp.stack([records[order.index(j)] for j in range(SHOTS)])
    gradient, traces = finish(info, terms, records)
    return (final[None], traces, gradient)


def solution(mesh):
    in_specs = (
        P(None, ("groups", "slab"), None),
        P(),
        P(),
        P(),
        P(("groups", "slab"), None, None, None),
        P(("groups", "slab"), None, None, None),
        P(None, ("groups", "slab"), None, None, None),
        P("groups", None),
        P("groups", None),
        P("groups", None, None),
    )
    out_specs = (
        P(("groups", "slab"), None, None, None),
        P("groups", None, None),
        P(("groups", "slab"), None),
    )
    return jax.shard_map(body, mesh=mesh, in_specs=in_specs, out_specs=out_specs, check_vma=False)
```

```python
import functools

import jax
import jax.numpy as jnp
import numpy as np
from jax import lax
from jax.experimental import pallas as pl
from jax.experimental.pallas import tpu as pltpu
from jax.sharding import PartitionSpec as P

CH = 64
CY = 32
CX = 64
FY = 64
FX = 128
CELLS = CY * CX
SHOTS = 8
STEPS = 4
NREC = 128
PLANES = 16
REACH = 4
CUR_RIM = REACH * STEPS
PREV_RIM = CUR_RIM - REACH
RIM_PLANES = CUR_RIM + PREV_RIM
PARTS = (0, 20, RIM_PLANES)
EXT = PLANES + 2 * CUR_RIM
PAD = 8
ROWS = FY + 2 * PAD
CHUNK = 4

stencil_weights = (-205.0 / 72.0, 8.0 / 5.0, -1.0 / 5.0, 8.0 / 315.0, -1.0 / 560.0)
lowest_speed = 1.5
speed_range = 3.0
courant = 0.088
leak_slope = 0.2

VMEM = pl.BlockSpec(memory_space=pltpu.VMEM)
ANY = pl.BlockSpec(memory_space=pl.ANY)
SMEM = pl.BlockSpec(memory_space=pltpu.SMEM)
PARAMS = pltpu.CompilerParams(vmem_limit_bytes=24 * 1024 * 1024)


def doubling_matrix(length):
    matrix = np.zeros((2 * length, length), np.float32)
    for k in range(length):
        matrix[2 * k, k] += 0.75
        matrix[2 * k, max(k - 1, 0)] += 0.25
        matrix[2 * k + 1, k] += 0.75
        matrix[2 * k + 1, min(k + 1, length - 1)] += 0.25
    return matrix


def plane_matrices():
    across = doubling_matrix(CX)
    down = doubling_matrix(CY)
    widen = np.zeros((128, 256), np.float32)
    widen[:64, :128] = across.T
    widen[64:, 128:] = across.T
    tall = np.concatenate([down[:, 0::2], down[:, 1::2]], axis=1)
    tall_twice = np.concatenate([tall, tall], axis=1)
    short_twice = np.concatenate([tall.T, tall.T], axis=1)
    narrow = widen.T
    return tuple(jnp.asarray(m, jnp.bfloat16) for m in (widen, tall_twice, short_twice, narrow))


def halves(value):
    high = value.astype(jnp.bfloat16)
    low = (value - high.astype(jnp.float32)).astype(jnp.bfloat16)
    return high, low


def leaky(value):
    return jnp.where(value > 0, value, leak_slope * value)


def conv(near_ref, mid_ref, far_ref, weight_ref, fields, packed):
    odd = lax.axis_index("slab") % 2
    depths = (2 - 2 * odd, 1, 2 * odd)
    column = lax.broadcasted_iota(jnp.int32, (CH, CELLS), 1) % CX
    for part, ref in enumerate((near_ref, mid_ref, far_ref)):
        plane = ref[...]
        wide = plane.astype(jnp.float32)
        left = jnp.where(column == 0, 0.0, pltpu.roll(wide, 1, 1)).astype(jnp.bfloat16)
        right = jnp.where(column == CX - 1, 0.0, pltpu.roll(wide, CELLS - 1, 1)).astype(jnp.bfloat16)
        for place, piece in enumerate((left, plane, right)):
            begin = (3 * part + place) * CH
            fields[begin : begin + CH, :] = piece
    for part, depth in enumerate(depths):
        for row in range(3):
            for place in range(3):
                begin = (3 * part + place) * CH
                packed[row * CH : (row + 1) * CH, begin : begin + CH] = weight_ref[
                    9 * depth + 3 * row + place
                ]
    products = jnp.dot(packed[...], fields[...], preferred_element_type=jnp.float32)
    cell = lax.broadcasted_iota(jnp.int32, (CH, CELLS), 1)
    above = jnp.where(cell < CX, 0.0, pltpu.roll(products[:CH], CX, 1))
    below = jnp.where(cell >= CELLS - CX, 0.0, pltpu.roll(products[2 * CH :], CELLS - CX, 1))
    return products[CH : 2 * CH] + above + below


def to_column(row):
    count = row.shape[1]
    here = lax.broadcasted_iota(jnp.int32, (count, count), 0)
    there = lax.broadcasted_iota(jnp.int32, (count, count), 1)
    return jnp.sum(jnp.where(here == there, row, 0), axis=1, keepdims=True)


def first_kernel(near_ref, mid_ref, far_ref, weight_ref, low_part, high_part, out_ref, fields, packed):
    out_ref[...] = leaky(conv(near_ref, mid_ref, far_ref, weight_ref, fields, packed)).astype(
        jnp.bfloat16
    )


def second_kernel(near_ref, mid_ref, far_ref, weight_ref, head_ref, low_part, high_part, out_ref, fields, packed):
    second = leaky(conv(near_ref, mid_ref, far_ref, weight_ref, fields, packed))
    head = to_column(head_ref[...].astype(jnp.float32))
    logits = jnp.sum(second * head, axis=0, keepdims=True)
    speed = lowest_speed + speed_range * jax.nn.sigmoid(logits)
    for j in range(16):
        out_ref[j : j + 1, :] = speed[:, 128 * j : 128 * (j + 1)].astype(jnp.bfloat16)


CONV_SCRATCH = [
    pltpu.VMEM((9 * CH, CELLS), jnp.bfloat16),
    pltpu.VMEM((3 * CH, 9 * CH), jnp.bfloat16),
]


def first_conv(near, mid, far, weight, low_part, high_part):
    return pl.pallas_call(
        first_kernel,
        out_shape=jax.ShapeDtypeStruct((CH, CELLS), jnp.bfloat16),
        in_specs=[VMEM] * 4 + [ANY] * 2,
        out_specs=VMEM,
        scratch_shapes=CONV_SCRATCH,
        compiler_params=PARAMS,
    )(near, mid, far, weight, low_part, high_part)


def second_conv(near, mid, far, weight, head, low_part, high_part):
    return pl.pallas_call(
        second_kernel,
        out_shape=jax.ShapeDtypeStruct((16, 128), jnp.bfloat16),
        in_specs=[VMEM] * 5 + [ANY] * 2,
        out_specs=VMEM,
        scratch_shapes=CONV_SCRATCH,
        compiler_params=PARAMS,
    )(near, mid, far, weight, head, low_part, high_part)


def band_matrix():
    band = np.zeros((FX, FX), np.float64)
    for reach, weight in enumerate(stencil_weights):
        for at in range(FX):
            if reach == 0:
                band[at, at] = 3.0 * weight
            elif at + reach < FX:
                band[at, at + reach] = band[at + reach, at] = weight
    high = band.astype(jnp.bfloat16)
    low = (band - high.astype(np.float64)).astype(jnp.bfloat16)
    return jnp.asarray(np.concatenate([high, high, low], axis=0))


INNER = slice(PAD, PAD + FY)


def laplace(field, first, band, use):
    planes = field[pl.ds(first, CHUNK), INNER, :].reshape(CHUNK * FY, FX)
    high, low = halves(planes)
    across = jnp.dot(
        jnp.concatenate([high, low, high], axis=1), band, preferred_element_type=jnp.float32
    )
    for row in range(0, FY, 8):
        column = [
            field[first + k - REACH, PAD + row : PAD + row + 8, :]
            for k in range(CHUNK + 2 * REACH)
        ]
        for k in range(CHUNK):
            total = across[k * FY + row : k * FY + row + 8]
            for reach in range(1, REACH + 1):
                near = column[k + REACH - reach] + column[k + REACH + reach]
                begin = PAD + row - reach
                near = near + field[first + k, begin : begin + 8, :]
                begin = PAD + row + reach
                near = near + field[first + k, begin : begin + 8, :]
                total = total + stencil_weights[reach] * near
            use(k, slice(row, row + 8), column[k + REACH], total)


def slab_place():
    slab = lax.axis_index("slab") // SHOTS
    slabs = lax.axis_size("slab") // SHOTS
    return slab, slab > 0, slab < slabs - 1


def clear_rows(field, first, last):
    def one(plane, _):
        field[plane, :PAD, :] = jnp.zeros((PAD, FX), jnp.float32)
        field[plane, PAD + FY :, :] = jnp.zeros((PAD, FX), jnp.float32)
        return 0

    lax.fori_loop(first, last, one, 0)


def clear_beyond(field, has_low, has_high):
    for inside, begin in ((has_low, CUR_RIM - REACH), (has_high, CUR_RIM + PLANES)):

        @pl.when(jnp.logical_not(inside))
        def _():
            for plane in range(begin, begin + REACH):
                field[plane, INNER, :] = jnp.zeros((FY, FX), jnp.float32)


def prepare_kernel(
    cur_ref,
    prev_ref,
    low_0,
    low_1,
    high_0,
    high_1,
    adjoint_ref,
    stations_ref,
    band_ref,
    cur_out,
    base_out,
    laplace_out,
    total_out,
    pick_out,
    field,
):
    slab, has_low, has_high = slab_place()
    band = band_ref[...]
    clear_rows(field, 0, EXT)
    clear_beyond(field, has_low, has_high)

    def load_own(plane, _):
        value = cur_ref[plane]
        field[CUR_RIM + plane, INNER, :] = value
        cur_out[CUR_RIM + plane] = value
        base_out[CUR_RIM + plane] = 2.0 * value - prev_ref[plane]
        return 0

    lax.fori_loop(0, PLANES, load_own, 0)

    def load_rim(parts, at_cur, at_prev):
        for ref, begin, end in zip(parts, PARTS[:-1], PARTS[1:]):

            def one(plane, _):
                value = ref[plane - begin].astype(jnp.float32)
                field[at_cur + plane - PREV_RIM, INNER, :] = value
                cur_out[at_cur + plane - PREV_RIM] = value
                return 0

            lax.fori_loop(max(begin, PREV_RIM), end, one, 0)
        for ref, begin, end in zip(parts, PARTS[:-1], PARTS[1:]):

            def two(plane, _):
                value = ref[plane - begin].astype(jnp.float32)
                base_out[at_prev + plane] = 2.0 * field[at_prev + plane, INNER, :] - value
                return 0

            lax.fori_loop(begin, min(end, PREV_RIM), two, 0)

    @pl.when(has_low)
    def _():
        load_rim((low_0, low_1), 0, REACH)

    @pl.when(has_high)
    def _():
        load_rim((high_0, high_1), CUR_RIM + PLANES, CUR_RIM + PLANES)

    def rim_planes(chunk, _):
        def use(k, rows, centre, lap):
            laplace_out[chunk * CHUNK + k, rows, :] = lap

        laplace(field, chunk * CHUNK, band, use)
        return 0

    def own_planes(chunk, _):
        def use(k, rows, centre, lap):
            laplace_out[CUR_RIM + chunk * CHUNK + k, rows, :] = lap
            weight = adjoint_ref[chunk * CHUNK + k, rows, :].astype(jnp.float32)
            total_out[chunk * CHUNK + k, rows, :] = weight * lap

        laplace(field, CUR_RIM + chunk * CHUNK, band, use)
        return 0

    first, last = stretch(has_low, has_high, PREV_RIM)
    lax.fori_loop(first // CHUNK, CUR_RIM // CHUNK, rim_planes, 0)
    lax.fori_loop(0, PLANES // CHUNK, own_planes, 0)
    lax.fori_loop((CUR_RIM + PLANES) // CHUNK, last // CHUNK, rim_planes, 0)

    shot = lax.axis_index("slab") % SHOTS
    depth = stations_ref[0, pl.ds(shot, 1), :] - slab * PLANES
    column = jnp.where((depth >= 0) & (depth < PLANES), stations_ref[2, pl.ds(shot, 1), :], -1)
    lane = lax.broadcasted_iota(jnp.int32, (NREC, FX), 1)
    pick_out[...] = jnp.where(to_column(column) == lane, 1.0, 0.0)


def stretch(has_low, has_high, reach_out):
    first = CUR_RIM - jnp.where(has_low, reach_out, 0)
    last = CUR_RIM + PLANES + jnp.where(has_high, reach_out, 0)
    return first, last


def prepare(*args):
    ext = jax.ShapeDtypeStruct((EXT, FY, FX), jnp.float32)
    return pl.pallas_call(
        prepare_kernel,
        out_shape=(
            ext,
            ext,
            ext,
            jax.ShapeDtypeStruct((PLANES, FY, FX), jnp.float32),
            jax.ShapeDtypeStruct((NREC, FX), jnp.float32),
        ),
        in_specs=[VMEM] * 9,
        out_specs=(VMEM,) * 5,
        scratch_shapes=[pltpu.VMEM((EXT, ROWS, FX), jnp.float32)],
        compiler_params=PARAMS,
    )(*args)


def wave_kernel(
    pulses,
    sources,
    stations,
    cur_ref,
    base_ref,
    laplace_ref,
    total_ref,
    pick_ref,
    adjoint_ref,
    own_speed,
    low_speed,
    high_speed,
    widen_ref,
    tall_ref,
    short_ref,
    narrow_ref,
    band_ref,
    final_ref,
    terms_ref,
    edges_ref,
    records_ref,
    field_a,
    field_b,
    factor,
    coarse,
    speed,
    total,
    rows_ref,
):
    shot = lax.axis_index("slab") % SHOTS
    slab, has_low, has_high = slab_place()
    band = band_ref[...]
    clear_rows(field_a, REACH, EXT - REACH)
    clear_rows(field_b, REACH, EXT - REACH)
    clear_beyond(field_a, has_low, has_high)
    clear_beyond(field_b, has_low, has_high)

    def widen_block(ref, at):
        block = ref[...].reshape(SHOTS * 16, 128)
        wide = jnp.dot(block, widen_ref[...], preferred_element_type=jnp.float32)
        for j in range(SHOTS):
            piece = wide[16 * j : 16 * (j + 1)]
            both = jnp.concatenate([piece[:, :128], piece[:, 128:]], axis=0)
            high, low = halves(both)
            stacked = jnp.concatenate([high, low], axis=0)
            coarse[at + (shot ^ j)] = jnp.dot(
                tall_ref[...], stacked, preferred_element_type=jnp.float32
            )

    widen_block(own_speed, SHOTS)

    @pl.when(has_low)
    def _():
        widen_block(low_speed, 0)

    @pl.when(jnp.logical_not(has_low))
    def _():
        coarse[SHOTS - 1] = coarse[SHOTS]

    @pl.when(has_high)
    def _():
        widen_block(high_speed, 2 * SHOTS)

    @pl.when(jnp.logical_not(has_high))
    def _():
        coarse[2 * SHOTS] = coarse[2 * SHOTS - 1]

    def refine(k, _):
        here = 0.75 * coarse[k]
        for plane, there in ((2 * k, coarse[k - 1]), (2 * k + 1, coarse[k + 1])):
            value = here + 0.25 * there
            square = (courant * value) * (courant * value)
            speed[plane] = value
            factor[plane] = square
            field_b[plane, INNER, :] = base_ref[plane] + square * laplace_ref[plane]
        return 0

    first, last = stretch(has_low, has_high, PREV_RIM)
    lax.fori_loop(first // 2, last // 2, refine, 0)

    source_plane = sources[0, shot] - slab * PLANES + CUR_RIM
    source_row = sources[1, shot]
    lane_row = lax.broadcasted_iota(jnp.int32, (1, FX), 1)

    def inject(field, pad, at, step, first, last):
        @pl.when((source_plane >= first) & (source_plane < last))
        def _():
            place = (source_plane - at, pl.ds(source_row + pad, 1), slice(None))
            field[place] = field[place] + jnp.where(
                lane_row == sources[2, shot], pulses[step, shot], 0.0
            )

    def collect(field, pad, at, step, k):
        depth = jnp.clip(stations[0, shot, k] - slab * PLANES, 0, PLANES - 1)
        rows_ref[step, pl.ds(k, 1), :] = field[
            depth + at, pl.ds(stations[1, shot, k] + pad, 1), :
        ]

    inject(field_b, PAD, 0, 0, first, last)

    for step in range(1, STEPS):
        now, before, out = (
            (field_b, cur_ref, field_a),
            (field_a, field_b, field_b),
            (field_b, field_a, final_ref),
        )[step - 1]
        reach_out = CUR_RIM - REACH * (step + 1)
        before_pad = 0 if before is cur_ref else PAD
        out_pad, out_at = (0, CUR_RIM) if out is final_ref else (PAD, 0)

        def advance(plane, rows, centre, lap):
            back = before[plane, rows.start + before_pad : rows.stop + before_pad, :]
            out[plane - out_at, rows.start + out_pad : rows.stop + out_pad, :] = (
                2.0 * centre - back + factor[plane, rows, :] * lap
            )

        def rim_planes(chunk, _):
            def use(k, rows, centre, lap):
                advance(chunk * CHUNK + k, rows, centre, lap)

            laplace(now, chunk * CHUNK, band, use)
            return 0

        def own_planes(chunk, _):
            begin = chunk * CHUNK

            def use(k, rows, centre, lap):
                weight = adjoint_ref[step, begin + k, rows, :].astype(jnp.float32)
                so_far = total_ref if step == 1 else total
                total[begin + k, rows, :] = so_far[begin + k, rows, :] + weight * lap
                advance(CUR_RIM + begin + k, rows, centre, lap)

            laplace(now, CUR_RIM + begin, band, use)
            share = NREC * CHUNK // PLANES
            for k in range(share):
                collect(now, PAD, CUR_RIM, step - 1, chunk * share + k)
            return 0

        first, last = stretch(has_low, has_high, reach_out)
        if reach_out > 0:
            lax.fori_loop(first // CHUNK, CUR_RIM // CHUNK, rim_planes, 0)
        lax.fori_loop(0, PLANES // CHUNK, own_planes, 0)
        if reach_out > 0:
            lax.fori_loop((CUR_RIM + PLANES) // CHUNK, last // CHUNK, rim_planes, 0)
        inject(out, out_pad, out_at, step, first, last)

    def collect_last(k, _):
        collect(final_ref, 0, 0, STEPS - 1, k)
        return 0

    lax.fori_loop(0, NREC, collect_last, 0, unroll=16)
    for step in range(STEPS):
        records_ref[step : step + 1, :] = jnp.sum(
            (rows_ref[step] * pick_ref[...]).T, axis=0, keepdims=True
        )

    def scale(plane, _):
        total[plane] = (2.0 * courant * courant) * speed[CUR_RIM + plane] * total[plane]
        return 0

    lax.fori_loop(0, PLANES, scale, 0)

    shrunk = []
    for k in range(-1, SHOTS + 1):
        value = 0.0
        for plane, weight in ((2 * k - 1, 0.25), (2 * k, 0.75), (2 * k + 1, 0.75), (2 * k + 2, 0.25)):
            if 0 <= plane < PLANES:
                value = value + weight * total[plane]
        high, low = halves(value)
        stacked = jnp.concatenate([high, low], axis=0)
        shrunk.append(jnp.dot(short_ref[...], stacked, preferred_element_type=jnp.float32))
    sides = [jnp.concatenate([z[:16], z[16:]], axis=1) for z in shrunk]
    high, low = halves(jnp.concatenate(sides, axis=0))
    narrow = narrow_ref[...]
    out = jnp.dot(high, narrow, preferred_element_type=jnp.float32) + jnp.dot(
        low, narrow, preferred_element_type=jnp.float32
    )
    below = out[:16]
    above = out[16 * (SHOTS + 1) :]
    for k in range(SHOTS):
        piece = out[16 * (k + 1) : 16 * (k + 2)]
        if k == 0:
            piece = piece + jnp.where(has_low, 0.0, below)
        if k == SHOTS - 1:
            piece = piece + jnp.where(has_high, 0.0, above)
        terms_ref[shot ^ k] = piece
    edges_ref[0] = jnp.where(has_low, below, 0.0)
    edges_ref[1] = jnp.where(has_high, above, 0.0)


def wave(*args):
    return pl.pallas_call(
        wave_kernel,
        out_shape=(
            jax.ShapeDtypeStruct((PLANES, FY, FX), jnp.float32),
            jax.ShapeDtypeStruct((SHOTS, 16, 128), jnp.float32),
            jax.ShapeDtypeStruct((2, 16, 128), jnp.float32),
            jax.ShapeDtypeStruct((STEPS, NREC), jnp.float32),
        ),
        in_specs=[SMEM] * 3 + [VMEM] * 14,
        out_specs=(VMEM,) * 4,
        scratch_shapes=[
            pltpu.VMEM((EXT, ROWS, FX), jnp.float32),
            pltpu.VMEM((EXT, ROWS, FX), jnp.float32),
            pltpu.VMEM((EXT, FY, FX), jnp.float32),
            pltpu.VMEM((3 * SHOTS, FY, FX), jnp.float32),
            pltpu.VMEM((EXT, FY, FX), jnp.float32),
            pltpu.VMEM((PLANES, FY, FX), jnp.float32),
            pltpu.VMEM((STEPS, NREC, FX), jnp.float32),
        ],
        compiler_params=PARAMS,
    )(*args)


def finish_kernel(term_ref, records_ref, gradient_ref, traces_ref):
    shot = lax.axis_index("slab") % SHOTS
    for j in range(16):
        gradient_ref[:, 128 * j : 128 * (j + 1)] = term_ref[j : j + 1, :]
    for j in range(SHOTS):
        traces_ref[shot ^ j] = records_ref[j]


def finish(term, records):
    return pl.pallas_call(
        finish_kernel,
        out_shape=(
            jax.ShapeDtypeStruct((1, CELLS), jnp.float32),
            jax.ShapeDtypeStruct((SHOTS, STEPS, NREC), jnp.float32),
        ),
        in_specs=[VMEM, VMEM],
        out_specs=(VMEM, VMEM),
        compiler_params=PARAMS,
    )(term, records)


def shift(value, steps):
    count = lax.axis_size("slab")
    begin, end = max(0, -steps), min(count, count - steps)
    return lax.ppermute(value, "slab", [(source, source + steps) for source in range(begin, end)])


def across_chips(value):
    count = lax.axis_size("slab")
    pairs = [(i, i + 1) for i in range(1, count - 1, 2)]
    return lax.ppermute(value, "slab", pairs + [(b, a) for a, b in pairs])


def partner(value, mask):
    count = lax.axis_size("slab")
    return lax.ppermute(value, "slab", [(source, source ^ mask) for source in range(count)])


def body(
    latent, conv1_weight, conv2_weight, head, p_prev, p_cur, adjoint, wavelet, sources, receivers
):
    position = lax.axis_index("slab")
    devices = lax.axis_size("slab")
    slabs = devices // SHOTS
    shot = position % SHOTS
    slab = position // SHOTS
    has_low = slab > 0
    has_high = slab < slabs - 1

    def exchange(to_low, to_high):
        if slabs == 2:
            got = partner(to_low if to_low is to_high else jnp.where(has_low, to_low, to_high), SHOTS)
            return got, got
        return shift(to_high, SHOTS), shift(to_low, -SHOTS)

    latent = latent.reshape(CH, CELLS)
    latent_far, latent_near = across_chips(latent), partner(latent, 1)
    current = p_cur[0]
    previous = p_prev[0]
    to_low = jnp.concatenate([previous[:PREV_RIM], current], axis=0).astype(jnp.bfloat16)
    to_high = jnp.concatenate([previous[PLANES - PREV_RIM :], current], axis=0).astype(jnp.bfloat16)
    to_low = [to_low[begin:end] for begin, end in zip(PARTS[:-1], PARTS[1:])]
    to_high = [to_high[begin:end] for begin, end in zip(PARTS[:-1], PARTS[1:])]
    low_0, high_0 = exchange(to_low[0], to_high[0])

    hidden = first_conv(latent_near, latent, latent_far, conv1_weight, latent_near, latent_near)
    hidden_far, hidden_near = across_chips(hidden), partner(hidden, 1)
    velocity = second_conv(
        hidden_near, hidden, hidden_far, conv2_weight, head[None], low_0, high_0
    )
    late = to_low[1], to_high[1]
    late, velocity_tied = lax.optimization_barrier((late, hidden_far))
    low_1, high_1 = exchange(*late)

    block = velocity[None]
    for bit in range(3):
        block = jnp.concatenate([block, partner(block, 1 << bit)], axis=0)
    block, low_1, high_1 = lax.optimization_barrier((block, low_1, high_1))
    speed_low, speed_high = exchange(block, block)

    stations = jnp.transpose(receivers, (1, 0, 2))
    adjoint = adjoint[:, 0]
    band = band_matrix()
    prepared = prepare(
        current,
        previous,
        low_0,
        low_1,
        high_0,
        high_1,
        adjoint[0],
        stations,
        band,
    )
    final, terms, edges, record = wave(
        wavelet.T,
        sources.T,
        stations,
        *prepared,
        adjoint,
        block,
        speed_low,
        speed_high,
        *plane_matrices(),
        band,
    )

    if slabs == 2:
        message = jnp.concatenate([jnp.where(has_low, edges[0], edges[1]), record], axis=0)
        got = partner(message, SHOTS)
        edge_low = jnp.where(has_low, got[:16], 0.0)
        edge_high = jnp.where(has_high, got[:16], 0.0)
        record = record + got[16:]
    else:
        edge_low, edge_high = shift(edges[1], SHOTS), shift(edges[0], -SHOTS)
        mask = SHOTS
        while mask < devices:
            record = record + partner(record, mask)
            mask *= 2
    place = jnp.arange(SHOTS)[:, None, None]
    terms = terms + jnp.where(place == shot, edge_low, 0.0)
    terms = terms + jnp.where(place == shot ^ (SHOTS - 1), edge_high, 0.0)
    terms = terms.reshape(SHOTS * 16, 128)
    records = record
    for bit in reversed(range(3)):
        half = terms.shape[0] // 2
        size = records.shape[0]
        got = partner(jnp.concatenate([terms[half:], records], axis=0), 1 << bit)
        terms = terms[:half] + got[:half]
        records = jnp.concatenate([records, got[half:]], axis=0)
    order = [4 * (j & 1) + (j & 2) + (j >> 2) for j in range(SHOTS)]
    records = records.reshape(SHOTS, STEPS, NREC)
    records = jnp.stack([records[order.index(j)] for j in range(SHOTS)])
    gradient, traces = finish(terms, records)
    return (final[None], traces, gradient)


def solution(mesh):
    in_specs = (
        P(None, ("groups", "slab"), None),
        P(),
        P(),
        P(),
        P(("groups", "slab"), None, None, None),
        P(("groups", "slab"), None, None, None),
        P(None, ("groups", "slab"), None, None, None),
        P("groups", None),
        P("groups", None),
        P("groups", None, None),
    )
    out_specs = (
        P(("groups", "slab"), None, None, None),
        P("groups", None, None),
        P(("groups", "slab"), None),
    )
    return jax.shard_map(body, mesh=mesh, in_specs=in_specs, out_specs=out_specs, check_vma=False)
```

```python
import functools

import jax
import jax.numpy as jnp
import numpy as np
from jax import lax
from jax.experimental import pallas as pl
from jax.experimental.pallas import tpu as pltpu
from jax.sharding import PartitionSpec as P

CH = 64
CY = 32
CX = 64
FY = 64
FX = 128
CELLS = CY * CX
SHOTS = 8
STEPS = 4
NREC = 128
PLANES = 16
REACH = 4
CUR_RIM = REACH * STEPS
PREV_RIM = CUR_RIM - REACH
RIM_PLANES = CUR_RIM + PREV_RIM
PARTS = (0, RIM_PLANES)
EXT = PLANES + 2 * CUR_RIM
PAD = 8
ROWS = FY + 2 * PAD
CHUNK = 4

stencil_weights = (-205.0 / 72.0, 8.0 / 5.0, -1.0 / 5.0, 8.0 / 315.0, -1.0 / 560.0)
lowest_speed = 1.5
speed_range = 3.0
courant = 0.088
leak_slope = 0.2

VMEM = pl.BlockSpec(memory_space=pltpu.VMEM)
ANY = pl.BlockSpec(memory_space=pl.ANY)
PARAMS = pltpu.CompilerParams(vmem_limit_bytes=24 * 1024 * 1024)


def doubling_matrix(length):
    matrix = np.zeros((2 * length, length), np.float32)
    for k in range(length):
        matrix[2 * k, k] += 0.75
        matrix[2 * k, max(k - 1, 0)] += 0.25
        matrix[2 * k + 1, k] += 0.75
        matrix[2 * k + 1, min(k + 1, length - 1)] += 0.25
    return matrix


def plane_matrices():
    across = doubling_matrix(CX)
    down = doubling_matrix(CY)
    widen = np.zeros((128, 256), np.float32)
    widen[:64, :128] = across.T
    widen[64:, 128:] = across.T
    tall = np.concatenate([down[:, 0::2], down[:, 1::2]], axis=1)
    tall_twice = np.concatenate([tall, tall], axis=1)
    short_twice = np.concatenate([tall.T, tall.T], axis=1)
    narrow = widen.T
    return tuple(jnp.asarray(m, jnp.bfloat16) for m in (widen, tall_twice, short_twice, narrow))


def halves(value):
    high = value.astype(jnp.bfloat16)
    low = (value - high.astype(jnp.float32)).astype(jnp.bfloat16)
    return high, low


def leaky(value):
    return jnp.where(value > 0, value, leak_slope * value)


def at_boundary():
    place = lax.axis_index("slab")
    rank = place % SHOTS
    last = lax.axis_size("slab") - 1
    return ((rank == 0) & (place > 0)) | ((rank == SHOTS - 1) & (place < last))


def conv(near, mid, far, weight_ref, fields, packed):
    odd = lax.axis_index("slab") % 2
    depths = (2 - 2 * odd, 1, 2 * odd)
    column = lax.broadcasted_iota(jnp.int32, (CH, CELLS), 1) % CX
    for part, plane in enumerate((near, mid, far)):
        wide = plane.astype(jnp.float32)
        left = jnp.where(column == 0, 0.0, pltpu.roll(wide, 1, 1)).astype(jnp.bfloat16)
        right = jnp.where(column == CX - 1, 0.0, pltpu.roll(wide, CELLS - 1, 1)).astype(jnp.bfloat16)
        for place, piece in enumerate((left, plane, right)):
            begin = (3 * part + place) * CH
            fields[begin : begin + CH, :] = piece
    for part, depth in enumerate(depths):
        for row in range(3):
            for place in range(3):
                begin = (3 * part + place) * CH
                packed[row * CH : (row + 1) * CH, begin : begin + CH] = weight_ref[
                    9 * depth + 3 * row + place
                ]
    products = jnp.dot(packed[...], fields[...], preferred_element_type=jnp.float32)
    cell = lax.broadcasted_iota(jnp.int32, (CH, CELLS), 1)
    above = jnp.where(cell < CX, 0.0, pltpu.roll(products[:CH], CX, 1))
    below = jnp.where(cell >= CELLS - CX, 0.0, pltpu.roll(products[2 * CH :], CELLS - CX, 1))
    return products[CH : 2 * CH] + above + below


def to_column(row):
    count = row.shape[1]
    here = lax.broadcasted_iota(jnp.int32, (count, count), 0)
    there = lax.broadcasted_iota(jnp.int32, (count, count), 1)
    return jnp.sum(jnp.where(here == there, row, 0), axis=1, keepdims=True)


def first_kernel(
    near_ref, mid_ref, far_ref, extra_ref, weight_ref, out_ref, beyond_ref, fields, packed
):
    near, mid, far = near_ref[...], mid_ref[...], far_ref[...]
    hidden = leaky(conv(near, mid, far, weight_ref, fields, packed))
    out_ref[...] = hidden.astype(jnp.bfloat16)

    @pl.when(at_boundary())
    def _():
        hidden = leaky(conv(mid, far, extra_ref[...], weight_ref, fields, packed))
        beyond_ref[...] = hidden.astype(jnp.bfloat16)


def second_kernel(
    near_ref, mid_ref, far_ref, beyond_ref, weight_ref, head_ref, out_ref, fields, packed
):
    far = jnp.where(at_boundary(), beyond_ref[...], far_ref[...])
    second = leaky(conv(near_ref[...], mid_ref[...], far, weight_ref, fields, packed))
    head = to_column(head_ref[...].astype(jnp.float32))
    logits = jnp.sum(second * head, axis=0, keepdims=True)
    speed = lowest_speed + speed_range * jax.nn.sigmoid(logits)
    for j in range(16):
        out_ref[j : j + 1, :] = speed[:, 128 * j : 128 * (j + 1)].astype(jnp.bfloat16)


CONV_SCRATCH = [
    pltpu.VMEM((9 * CH, CELLS), jnp.bfloat16),
    pltpu.VMEM((3 * CH, 9 * CH), jnp.bfloat16),
]


def first_conv(near, mid, far, extra, weight):
    plane = jax.ShapeDtypeStruct((CH, CELLS), jnp.bfloat16)
    return pl.pallas_call(
        first_kernel,
        out_shape=(plane, plane),
        in_specs=[VMEM] * 5,
        out_specs=(VMEM, VMEM),
        scratch_shapes=CONV_SCRATCH,
        compiler_params=PARAMS,
    )(near, mid, far, extra, weight)


def second_conv(near, mid, far, beyond, weight, head):
    return pl.pallas_call(
        second_kernel,
        out_shape=jax.ShapeDtypeStruct((16, 128), jnp.bfloat16),
        in_specs=[VMEM] * 6,
        out_specs=VMEM,
        scratch_shapes=CONV_SCRATCH,
        compiler_params=PARAMS,
    )(near, mid, far, beyond, weight, head)


def band_matrix():
    band = np.zeros((FX, FX), np.float64)
    for reach, weight in enumerate(stencil_weights):
        for at in range(FX):
            if reach == 0:
                band[at, at] = 3.0 * weight
            elif at + reach < FX:
                band[at, at + reach] = band[at + reach, at] = weight
    high = band.astype(jnp.bfloat16)
    low = (band - high.astype(np.float64)).astype(jnp.bfloat16)
    return jnp.asarray(np.block([[high, low], [high, np.zeros_like(low)]]))


INNER = slice(PAD, PAD + FY)


def laplace(field, first, band, use):
    planes = field[pl.ds(first, CHUNK), INNER, :].reshape(CHUNK * FY, FX)
    high, low = halves(planes)
    across = jnp.dot(
        jnp.concatenate([high, low], axis=1), band, preferred_element_type=jnp.float32
    )
    for row in range(0, FY, 8):
        column = [
            field[first + k - REACH, PAD + row : PAD + row + 8, :]
            for k in range(CHUNK + 2 * REACH)
        ]
        for k in range(CHUNK):
            begin = k * FY + row
            total = across[begin : begin + 8, :FX] + across[begin : begin + 8, FX:]
            for reach in range(1, REACH + 1):
                near = column[k + REACH - reach] + column[k + REACH + reach]
                begin = PAD + row - reach
                near = near + field[first + k, begin : begin + 8, :]
                begin = PAD + row + reach
                near = near + field[first + k, begin : begin + 8, :]
                total = total + stencil_weights[reach] * near
            use(k, slice(row, row + 8), column[k + REACH], total)


def slab_place():
    slab = lax.axis_index("slab") // SHOTS
    slabs = lax.axis_size("slab") // SHOTS
    return slab, slab > 0, slab < slabs - 1


def over_rims(has_low, has_high, planes, size, use):
    count = planes // size
    below, above = CUR_RIM // size - count, (CUR_RIM + PLANES) // size
    if lax.axis_size("slab") == 2 * SHOTS:
        for k in range(count):
            use(jnp.where(has_low, below, above) + k)
        return
    for inside, begin in ((has_low, below), (has_high, above)):

        @pl.when(inside)
        def _():
            for k in range(count):
                use(begin + k)


def clear_rows(field, first, last):
    def one(plane, _):
        field[plane, :PAD, :] = jnp.zeros((PAD, FX), jnp.float32)
        field[plane, PAD + FY :, :] = jnp.zeros((PAD, FX), jnp.float32)
        return 0

    lax.fori_loop(first, last, one, 0, unroll=8)


def clear_beyond(field, has_low, has_high):
    for inside, begin in ((has_low, CUR_RIM - REACH), (has_high, CUR_RIM + PLANES)):

        @pl.when(jnp.logical_not(inside))
        def _():
            for plane in range(begin, begin + REACH):
                field[plane, INNER, :] = jnp.zeros((FY, FX), jnp.float32)


def plan_kernel(stations_ref, sources_ref, pulses_ref, plan_out, pick_out, pulses_out):
    slab, _, _ = slab_place()
    shot = lax.axis_index("slab") % SHOTS
    depth = stations_ref[0, pl.ds(shot, 1), :] - slab * PLANES
    inside = (depth >= 0) & (depth < PLANES)
    column = jnp.where(inside, stations_ref[2, pl.ds(shot, 1), :], -1)
    lane = lax.broadcasted_iota(jnp.int32, (NREC, FX), 1)
    pick_out[...] = jnp.where(to_column(column) == lane, 1.0, 0.0)
    plan_out[:1, :] = (
        (jnp.clip(depth, 0, PLANES - 1) + CUR_RIM) * ROWS + PAD + stations_ref[1, pl.ds(shot, 1), :]
    )
    mine = lax.broadcasted_iota(jnp.int32, (1, SHOTS), 1) == shot
    source = jnp.sum(jnp.where(mine, sources_ref[...], 0), axis=1, keepdims=True)
    plan_out[1:2, :] = jnp.broadcast_to(source[:1] - slab * PLANES + CUR_RIM, (1, FX))
    plan_out[2:3, :] = jnp.broadcast_to(source[1:2] + PAD, (1, FX))
    plan_out[3:4, :] = jnp.broadcast_to(source[2:], (1, FX))
    pulse = jnp.sum(jnp.where(mine, pulses_ref[...], 0.0), axis=1, keepdims=True)
    pulses_out[...] = jnp.broadcast_to(pulse, (STEPS, FX))


def plan_wave(stations, sources, pulses):
    return pl.pallas_call(
        plan_kernel,
        out_shape=(
            jax.ShapeDtypeStruct((4, NREC), jnp.int32),
            jax.ShapeDtypeStruct((NREC, FX), jnp.float32),
            jax.ShapeDtypeStruct((STEPS, FX), jnp.float32),
        ),
        in_specs=[VMEM] * 3,
        out_specs=(VMEM,) * 3,
        compiler_params=PARAMS,
    )(stations, sources, pulses)


def stretch(has_low, has_high, reach_out):
    first = CUR_RIM - jnp.where(has_low, reach_out, 0)
    last = CUR_RIM + PLANES + jnp.where(has_high, reach_out, 0)
    return first, last


def wave_kernel(
    plan,
    pick_ref,
    pulses_ref,
    cur_ref,
    prev_ref,
    low_0,
    high_0,
    adjoint_ref,
    speeds_ref,
    widen_ref,
    tall_ref,
    short_ref,
    narrow_ref,
    band_ref,
    final_out,
    terms_ref,
    copied,
    field_a,
    field_b,
    factor,
    coarse,
    speed,
    total,
    rows_ref,
):
    slab, has_low, has_high = slab_place()
    band = band_ref[...]
    for field in (field_a, field_b):
        clear_rows(field, 0, EXT)
        clear_beyond(field, has_low, has_high)

    for plane in range(PLANES):
        value = cur_ref[plane]
        field_a[CUR_RIM + plane, INNER, :] = value
        field_b[CUR_RIM + plane, INNER, :] = 2.0 * value - prev_ref[plane]

    def load_rim(parts, at_cur, at_prev):
        def rim(plane):
            for ref, begin, end in zip(parts, PARTS[:-1], PARTS[1:]):
                if begin <= plane < end:
                    return ref[plane - begin].astype(jnp.float32)

        for plane in range(CUR_RIM):
            field_a[at_cur + plane, INNER, :] = rim(PREV_RIM + plane)
        for plane in range(PREV_RIM):
            field_b[at_prev + plane, INNER, :] = 2.0 * field_a[
                at_prev + plane, INNER, :
            ] - rim(plane)

    @pl.when(has_low)
    def _():
        load_rim((low_0,), 0, REACH)

    @pl.when(has_high)
    def _():
        load_rim((high_0,), CUR_RIM + PLANES, CUR_RIM + PLANES)

    def widen_block(slab, at):
        block = speeds_ref[pl.ds(slab * SHOTS, SHOTS)].reshape(SHOTS * 16, 128)
        wide = jnp.dot(block, widen_ref[...], preferred_element_type=jnp.float32)
        for k in range(SHOTS):
            piece = wide[16 * k : 16 * (k + 1)]
            both = jnp.concatenate([piece[:, :128], piece[:, 128:]], axis=0)
            high, low = halves(both)
            stacked = jnp.concatenate([high, low], axis=0)
            coarse[at + k] = jnp.dot(
                tall_ref[...], stacked, preferred_element_type=jnp.float32
            )

    widen_block(slab, SHOTS)

    @pl.when(has_low)
    def _():
        widen_block(slab - 1, 0)

    @pl.when(jnp.logical_not(has_low))
    def _():
        coarse[SHOTS - 1] = coarse[SHOTS]

    @pl.when(has_high)
    def _():
        widen_block(slab + 1, 2 * SHOTS)

    @pl.when(jnp.logical_not(has_high))
    def _():
        coarse[2 * SHOTS] = coarse[2 * SHOTS - 1]

    def refine(k):
        here = 0.75 * coarse[k]
        for plane, there in ((2 * k, coarse[k - 1]), (2 * k + 1, coarse[k + 1])):
            value = here + 0.25 * there
            speed[plane] = value
            factor[plane] = (courant * value) * (courant * value)

    for k in range(CUR_RIM // 2, (CUR_RIM + PLANES) // 2):
        refine(k)
    over_rims(has_low, has_high, PREV_RIM, 2, refine)

    source_plane, source_row = plan[1, 0], plan[2, 0]
    lane_row = lax.broadcasted_iota(jnp.int32, (1, FX), 1)

    def inject(field, step, first, last):
        @pl.when((source_plane >= first) & (source_plane < last))
        def _():
            place = (source_plane, pl.ds(source_row, 1), slice(None))
            field[place] = field[place] + jnp.where(
                lane_row == plan[3, 0], pulses_ref[step : step + 1, :], 0.0
            )

    def collect(field, step, k):
        rows_ref[step, pl.ds(k, 1), :] = field.reshape(EXT * ROWS, FX)[pl.ds(plan[0, k], 1), :]

    for step in range(STEPS):
        now, out = (field_a, field_b) if step % 2 == 0 else (field_b, field_a)
        reach_out = CUR_RIM - REACH * (step + 1)

        def advance(plane, rows, centre, lap):
            here = (plane, slice(rows.start + PAD, rows.stop + PAD), slice(None))
            carried = out[here] if step == 0 else 2.0 * centre - out[here]
            out[here] = carried + factor[plane, rows, :] * lap

        def rim_planes(chunk):
            def use(k, rows, centre, lap):
                advance(chunk * CHUNK + k, rows, centre, lap)

            laplace(now, chunk * CHUNK, band, use)

        def own_planes(chunk):
            begin = chunk * CHUNK

            def use(k, rows, centre, lap):
                term = adjoint_ref[step, begin + k, rows, :].astype(jnp.float32) * lap
                if step > 0:
                    term = total[begin + k, rows, :] + term
                total[begin + k, rows, :] = term
                advance(CUR_RIM + begin + k, rows, centre, lap)

            laplace(now, CUR_RIM + begin, band, use)
            share = NREC * CHUNK // PLANES if step > 0 else 0
            for k in range(share):
                collect(now, step - 1, chunk * share + k)

        first, last = stretch(has_low, has_high, reach_out)
        for chunk in range(PLANES // CHUNK):
            own_planes(chunk)
        if reach_out > 0:
            over_rims(has_low, has_high, reach_out, CHUNK, rim_planes)
        inject(out, step, first, last)

    store = pltpu.make_async_copy(
        field_a.at[pl.ds(CUR_RIM, PLANES), pl.ds(PAD, FY), :], final_out, copied
    )
    store.start()
    for k in range(NREC):
        collect(field_a, STEPS - 1, k)
    record = jnp.concatenate(
        [
            jnp.sum((rows_ref[step] * pick_ref[...]).T, axis=0, keepdims=True)
            for step in range(STEPS)
        ]
        + [jnp.zeros((16 - STEPS, FX), jnp.float32)],
        axis=0,
    ).astype(jnp.bfloat16)

    for plane in range(PLANES):
        total[plane] = (2.0 * courant * courant) * speed[CUR_RIM + plane] * total[plane]

    shrunk = []
    for k in range(-1, SHOTS + 1):
        value = 0.0
        for plane, weight in ((2 * k - 1, 0.25), (2 * k, 0.75), (2 * k + 1, 0.75), (2 * k + 2, 0.25)):
            if 0 <= plane < PLANES:
                value = value + weight * total[plane]
        high, low = halves(value)
        stacked = jnp.concatenate([high, low], axis=0)
        shrunk.append(jnp.dot(short_ref[...], stacked, preferred_element_type=jnp.float32))
    sides = [jnp.concatenate([z[:16], z[16:]], axis=1) for z in shrunk]
    high, low = halves(jnp.concatenate(sides, axis=0))
    narrow = narrow_ref[...]
    out = jnp.dot(high, narrow, preferred_element_type=jnp.float32) + jnp.dot(
        low, narrow, preferred_element_type=jnp.float32
    )
    below = out[:16]
    above = out[16 * (SHOTS + 1) :]

    def no_term(position, _):
        terms_ref[position, :16, :] = jnp.zeros((16, 128), jnp.bfloat16)
        terms_ref[position, 16:, :] = record
        return 0

    lax.fori_loop(0, terms_ref.shape[0], no_term, 0, unroll=8)
    for k in range(SHOTS):
        piece = out[16 * (k + 1) : 16 * (k + 2)]
        if k == 0:
            piece = piece + jnp.where(has_low, 0.0, below)
        if k == SHOTS - 1:
            piece = piece + jnp.where(has_high, 0.0, above)
        terms_ref[slab * SHOTS + k, :16, :] = piece.astype(jnp.bfloat16)

    @pl.when(has_low)
    def _():
        terms_ref[slab * SHOTS - 1, :16, :] = below.astype(jnp.bfloat16)

    @pl.when(has_high)
    def _():
        terms_ref[slab * SHOTS + SHOTS, :16, :] = above.astype(jnp.bfloat16)

    store.wait()


def wave(*args):
    devices = lax.axis_size("slab")
    return pl.pallas_call(
        wave_kernel,
        out_shape=(
            jax.ShapeDtypeStruct((PLANES, FY, FX), jnp.float32),
            jax.ShapeDtypeStruct((devices, 32, 128), jnp.bfloat16),
        ),
        in_specs=[pl.BlockSpec(memory_space=pltpu.SMEM)] + [VMEM] * 13,
        out_specs=(ANY, VMEM),
        scratch_shapes=[
            pltpu.SemaphoreType.DMA,
            pltpu.VMEM((EXT, ROWS, FX), jnp.float32),
            pltpu.VMEM((EXT, ROWS, FX), jnp.float32),
            pltpu.VMEM((EXT, FY, FX), jnp.float32),
            pltpu.VMEM((3 * SHOTS, FY, FX), jnp.float32),
            pltpu.VMEM((EXT, FY, FX), jnp.float32),
            pltpu.VMEM((PLANES, FY, FX), jnp.float32),
            pltpu.VMEM((STEPS, NREC, FX), jnp.float32),
        ],
        compiler_params=PARAMS,
    )(*args)


def finish_kernel(terms_ref, gradient_ref, traces_ref):
    devices = terms_ref.shape[0]
    term = terms_ref[0, :16, :].astype(jnp.float32)
    for position in range(1, devices):
        term = term + terms_ref[position, :16, :].astype(jnp.float32)
    for j in range(16):
        gradient_ref[:, 128 * j : 128 * (j + 1)] = term[j : j + 1, :]
    for shot in range(SHOTS):
        record = terms_ref[shot, 16:, :].astype(jnp.float32)
        for position in range(shot + SHOTS, devices, SHOTS):
            record = record + terms_ref[position, 16:, :].astype(jnp.float32)
        traces_ref[shot] = record[:STEPS]


def finish(terms):
    return pl.pallas_call(
        finish_kernel,
        out_shape=(
            jax.ShapeDtypeStruct((1, CELLS), jnp.float32),
            jax.ShapeDtypeStruct((SHOTS, STEPS, NREC), jnp.float32),
        ),
        in_specs=[VMEM],
        out_specs=(VMEM, VMEM),
        compiler_params=PARAMS,
    )(terms)


def shift(value, steps):
    count = lax.axis_size("slab")
    begin, end = max(0, -steps), min(count, count - steps)
    return lax.ppermute(value, "slab", [(source, source + steps) for source in range(begin, end)])


def across_chips(value, boundaries):
    count = lax.axis_size("slab")
    pairs = [(i, i + 1) for i in range(1, count - 1, 2) if boundaries or (i + 1) % SHOTS > 0]
    return lax.ppermute(value, "slab", pairs + [(b, a) for a, b in pairs])


def past_boundary(value):
    pairs = []
    for first in range(SHOTS, lax.axis_size("slab"), SHOTS):
        pairs += [(first + 1, first - 1), (first - 2, first)]
    return lax.ppermute(value, "slab", pairs)


def partner(value, mask):
    count = lax.axis_size("slab")
    return lax.ppermute(value, "slab", [(source, source ^ mask) for source in range(count)])


def body(
    latent, conv1_weight, conv2_weight, head, p_prev, p_cur, adjoint, wavelet, sources, receivers
):
    position = lax.axis_index("slab")
    devices = lax.axis_size("slab")
    slabs = devices // SHOTS
    shot = position % SHOTS
    slab = position // SHOTS
    has_low = slab > 0
    has_high = slab < slabs - 1

    def exchange(to_low, to_high):
        if slabs == 2:
            got = partner(to_low if to_low is to_high else jnp.where(has_low, to_low, to_high), SHOTS)
            return got, got
        return shift(to_high, SHOTS), shift(to_low, -SHOTS)

    latent = latent.reshape(CH, CELLS)
    latent_far, latent_near = across_chips(latent, True), partner(latent, 1)
    latent_extra = past_boundary(latent)
    current = p_cur[0]
    previous = p_prev[0]
    to_low = jnp.concatenate([previous[:PREV_RIM], current], axis=0).astype(jnp.bfloat16)
    to_high = jnp.concatenate([previous[PLANES - PREV_RIM :], current], axis=0).astype(jnp.bfloat16)
    to_low = [to_low[begin:end] for begin, end in zip(PARTS[:-1], PARTS[1:])]
    to_high = [to_high[begin:end] for begin, end in zip(PARTS[:-1], PARTS[1:])]
    to_low, to_high, _ = lax.optimization_barrier(
        (to_low[0], to_high[0], (latent_far, latent_near, latent_extra))
    )
    low_0, high_0 = exchange(to_low, to_high)

    hidden, beyond = first_conv(latent_near, latent, latent_far, latent_extra, conv1_weight)
    hidden_far, hidden_near = across_chips(hidden, False), partner(hidden, 1)
    velocity = second_conv(hidden_near, hidden, hidden_far, beyond, conv2_weight, head[None])
    speeds = lax.all_to_all(
        jnp.broadcast_to(velocity[None], (devices,) + velocity.shape), "slab", 0, 0
    )

    adjoint = adjoint[:, 0]
    plan, pick, pulses = plan_wave(
        jnp.transpose(receivers, (1, 0, 2)), sources.T, wavelet.T
    )
    final, terms = wave(
        plan,
        pick,
        pulses,
        current,
        previous,
        low_0,
        high_0,
        adjoint,
        speeds,
        *plane_matrices(),
        band_matrix(),
    )

    gradient, traces = finish(lax.all_to_all(terms, "slab", 0, 0))
    return (final[None], traces, gradient)


def solution(mesh):
    in_specs = (
        P(None, ("groups", "slab"), None),
        P(),
        P(),
        P(),
        P(("groups", "slab"), None, None, None),
        P(("groups", "slab"), None, None, None),
        P(None, ("groups", "slab"), None, None, None),
        P("groups", None),
        P("groups", None),
        P("groups", None, None),
    )
    out_specs = (
        P(("groups", "slab"), None, None, None),
        P("groups", None, None),
        P(("groups", "slab"), None),
    )
    return jax.shard_map(body, mesh=mesh, in_specs=in_specs, out_specs=out_specs, check_vma=False)
```

```python
import functools

import jax
import jax.numpy as jnp
import numpy as np
from jax import lax
from jax.experimental import pallas as pl
from jax.experimental.pallas import tpu as pltpu
from jax.sharding import PartitionSpec as P

CH = 64
CY = 32
CX = 64
FY = 64
FX = 128
CELLS = CY * CX
SHOTS = 8
STEPS = 4
NREC = 128
PLANES = 16
REACH = 4
CUR_RIM = REACH * STEPS
PREV_RIM = CUR_RIM - REACH
RIM_PLANES = CUR_RIM + PREV_RIM
PARTS = (0, RIM_PLANES)
EXT = PLANES + 2 * CUR_RIM
PAD = 8
ROWS = FY + 2 * PAD
CHUNK = 4

stencil_weights = (-205.0 / 72.0, 8.0 / 5.0, -1.0 / 5.0, 8.0 / 315.0, -1.0 / 560.0)
lowest_speed = 1.5
speed_range = 3.0
courant = 0.088
leak_slope = 0.2

VMEM = pl.BlockSpec(memory_space=pltpu.VMEM)
ANY = pl.BlockSpec(memory_space=pl.ANY)
PARAMS = pltpu.CompilerParams(vmem_limit_bytes=24 * 1024 * 1024)


def doubling_matrix(length):
    matrix = np.zeros((2 * length, length), np.float32)
    for k in range(length):
        matrix[2 * k, k] += 0.75
        matrix[2 * k, max(k - 1, 0)] += 0.25
        matrix[2 * k + 1, k] += 0.75
        matrix[2 * k + 1, min(k + 1, length - 1)] += 0.25
    return matrix


def plane_matrices():
    across = doubling_matrix(CX)
    down = doubling_matrix(CY)
    widen = np.zeros((128, 256), np.float32)
    widen[:64, :128] = across.T
    widen[64:, 128:] = across.T
    tall = np.concatenate([down[:, 0::2], down[:, 1::2]], axis=1)
    tall_twice = np.concatenate([tall, tall], axis=1)
    short_twice = np.concatenate([tall.T, tall.T], axis=1)
    narrow = widen.T
    return tuple(jnp.asarray(m, jnp.bfloat16) for m in (widen, tall_twice, short_twice, narrow))


def halves(value):
    high = value.astype(jnp.bfloat16)
    low = (value - high.astype(jnp.float32)).astype(jnp.bfloat16)
    return high, low


def leaky(value):
    return jnp.where(value > 0, value, leak_slope * value)


def at_boundary():
    place = lax.axis_index("slab")
    rank = place % SHOTS
    last = lax.axis_size("slab") - 1
    return ((rank == 0) & (place > 0)) | ((rank == SHOTS - 1) & (place < last))


def conv(near, mid, far, weight_ref, fields, packed):
    odd = lax.axis_index("slab") % 2
    depths = (2 - 2 * odd, 1, 2 * odd)
    column = lax.broadcasted_iota(jnp.int32, (CH, CELLS), 1) % CX
    for part, plane in enumerate((near, mid, far)):
        wide = plane.astype(jnp.float32)
        left = jnp.where(column == 0, 0.0, pltpu.roll(wide, 1, 1)).astype(jnp.bfloat16)
        right = jnp.where(column == CX - 1, 0.0, pltpu.roll(wide, CELLS - 1, 1)).astype(jnp.bfloat16)
        for place, piece in enumerate((left, plane, right)):
            begin = (3 * part + place) * CH
            fields[begin : begin + CH, :] = piece
    for part, depth in enumerate(depths):
        for row in range(3):
            for place in range(3):
                begin = (3 * part + place) * CH
                packed[row * CH : (row + 1) * CH, begin : begin + CH] = weight_ref[
                    9 * depth + 3 * row + place
                ]
    products = jnp.dot(packed[...], fields[...], preferred_element_type=jnp.float32)
    cell = lax.broadcasted_iota(jnp.int32, (CH, CELLS), 1)
    above = jnp.where(cell < CX, 0.0, pltpu.roll(products[:CH], CX, 1))
    below = jnp.where(cell >= CELLS - CX, 0.0, pltpu.roll(products[2 * CH :], CELLS - CX, 1))
    return products[CH : 2 * CH] + above + below


def to_column(row):
    count = row.shape[1]
    here = lax.broadcasted_iota(jnp.int32, (count, count), 0)
    there = lax.broadcasted_iota(jnp.int32, (count, count), 1)
    return jnp.sum(jnp.where(here == there, row, 0), axis=1, keepdims=True)


def first_kernel(
    near_ref, mid_ref, far_ref, extra_ref, weight_ref, out_ref, beyond_ref, fields, packed
):
    near, mid, far = near_ref[...], mid_ref[...], far_ref[...]
    hidden = leaky(conv(near, mid, far, weight_ref, fields, packed))
    out_ref[...] = hidden.astype(jnp.bfloat16)

    @pl.when(at_boundary())
    def _():
        hidden = leaky(conv(mid, far, extra_ref[...], weight_ref, fields, packed))
        beyond_ref[...] = hidden.astype(jnp.bfloat16)


def second_kernel(
    near_ref, mid_ref, far_ref, beyond_ref, weight_ref, head_ref, out_ref, fields, packed
):
    far = jnp.where(at_boundary(), beyond_ref[...], far_ref[...])
    second = leaky(conv(near_ref[...], mid_ref[...], far, weight_ref, fields, packed))
    head = to_column(head_ref[...].astype(jnp.float32))
    logits = jnp.sum(second * head, axis=0, keepdims=True)
    speed = lowest_speed + speed_range * jax.nn.sigmoid(logits)
    for j in range(16):
        out_ref[j : j + 1, :] = speed[:, 128 * j : 128 * (j + 1)].astype(jnp.bfloat16)


CONV_SCRATCH = [
    pltpu.VMEM((9 * CH, CELLS), jnp.bfloat16),
    pltpu.VMEM((3 * CH, 9 * CH), jnp.bfloat16),
]


def first_conv(near, mid, far, extra, weight):
    plane = jax.ShapeDtypeStruct((CH, CELLS), jnp.bfloat16)
    return pl.pallas_call(
        first_kernel,
        out_shape=(plane, plane),
        in_specs=[VMEM] * 5,
        out_specs=(VMEM, VMEM),
        scratch_shapes=CONV_SCRATCH,
        compiler_params=PARAMS,
    )(near, mid, far, extra, weight)


def second_conv(near, mid, far, beyond, weight, head):
    return pl.pallas_call(
        second_kernel,
        out_shape=jax.ShapeDtypeStruct((16, 128), jnp.bfloat16),
        in_specs=[VMEM] * 6,
        out_specs=VMEM,
        scratch_shapes=CONV_SCRATCH,
        compiler_params=PARAMS,
    )(near, mid, far, beyond, weight, head)


def band_matrix(length, diagonal):
    band = np.zeros((length, length), np.float64)
    for reach, weight in enumerate(stencil_weights):
        for at in range(length):
            if reach == 0:
                band[at, at] = diagonal
            elif at + reach < length:
                band[at, at + reach] = band[at + reach, at] = weight
    high = band.astype(jnp.bfloat16)
    return high, (band - high.astype(np.float64)).astype(jnp.bfloat16)


def row_band():
    high, low = band_matrix(FX, 3.0 * stencil_weights[0])
    return jnp.asarray(np.block([[high, low], [high, np.zeros_like(low)]]))


def column_band():
    high, low = band_matrix(FY, 0.0)
    return jnp.asarray(np.concatenate([high, high, low], axis=1))


INNER = slice(PAD, PAD + FY)


def laplace(field, first, bands, use):
    planes = field[pl.ds(first, CHUNK), INNER, :].reshape(CHUNK * FY, FX)
    high, low = halves(planes)
    across = jnp.dot(
        jnp.concatenate([high, low], axis=1), bands[0][...], preferred_element_type=jnp.float32
    )

    def abreast(value):
        return jnp.concatenate([value[k * FY : (k + 1) * FY] for k in range(CHUNK)], axis=1)

    high, low = abreast(high), abreast(low)
    down = jnp.dot(
        bands[1][...],
        jnp.concatenate([high, low, high], axis=0),
        preferred_element_type=jnp.float32,
    )
    for row in range(0, FY, 8):
        column = [
            field[first + k - REACH, PAD + row : PAD + row + 8, :]
            for k in range(CHUNK + 2 * REACH)
        ]
        for k in range(CHUNK):
            begin = k * FY + row
            total = across[begin : begin + 8, :FX] + across[begin : begin + 8, FX:]
            total = total + down[row : row + 8, k * FX : (k + 1) * FX]
            for reach in range(1, REACH + 1):
                near = column[k + REACH - reach] + column[k + REACH + reach]
                total = total + stencil_weights[reach] * near
            use(k, slice(row, row + 8), column[k + REACH], total)


def slab_place():
    slab = lax.axis_index("slab") // SHOTS
    slabs = lax.axis_size("slab") // SHOTS
    return slab, slab > 0, slab < slabs - 1


def over_rims(has_low, has_high, planes, size, use):
    count = planes // size
    below, above = CUR_RIM // size - count, (CUR_RIM + PLANES) // size
    if lax.axis_size("slab") == 2 * SHOTS:
        for k in range(count):
            use(jnp.where(has_low, below, above) + k)
        return
    for inside, begin in ((has_low, below), (has_high, above)):

        @pl.when(inside)
        def _():
            for k in range(count):
                use(begin + k)


def clear_rows(field, first, last):
    def one(plane, _):
        field[plane, :PAD, :] = jnp.zeros((PAD, FX), jnp.float32)
        field[plane, PAD + FY :, :] = jnp.zeros((PAD, FX), jnp.float32)
        return 0

    lax.fori_loop(first, last, one, 0, unroll=8)


def clear_beyond(field, has_low, has_high):
    for inside, begin in ((has_low, CUR_RIM - REACH), (has_high, CUR_RIM + PLANES)):

        @pl.when(jnp.logical_not(inside))
        def _():
            for plane in range(begin, begin + REACH):
                field[plane, INNER, :] = jnp.zeros((FY, FX), jnp.float32)


def plan_kernel(stations_ref, sources_ref, pulses_ref, plan_out, pick_out, pulses_out):
    slab, _, _ = slab_place()
    shot = lax.axis_index("slab") % SHOTS
    depth = stations_ref[0, pl.ds(shot, 1), :] - slab * PLANES
    inside = (depth >= 0) & (depth < PLANES)
    column = jnp.where(inside, stations_ref[2, pl.ds(shot, 1), :], -1)
    lane = lax.broadcasted_iota(jnp.int32, (NREC, FX), 1)
    pick_out[...] = jnp.where(to_column(column) == lane, 1.0, 0.0)
    plan_out[:1, :] = (
        (jnp.clip(depth, 0, PLANES - 1) + CUR_RIM) * ROWS + PAD + stations_ref[1, pl.ds(shot, 1), :]
    )
    mine = lax.broadcasted_iota(jnp.int32, (1, SHOTS), 1) == shot
    source = jnp.sum(jnp.where(mine, sources_ref[...], 0), axis=1, keepdims=True)
    plan_out[1:2, :] = jnp.broadcast_to(source[:1] - slab * PLANES + CUR_RIM, (1, FX))
    plan_out[2:3, :] = jnp.broadcast_to(source[1:2] + PAD, (1, FX))
    plan_out[3:4, :] = jnp.broadcast_to(source[2:], (1, FX))
    pulse = jnp.sum(jnp.where(mine, pulses_ref[...], 0.0), axis=1, keepdims=True)
    pulses_out[...] = jnp.broadcast_to(pulse, (STEPS, FX))


def plan_wave(stations, sources, pulses):
    return pl.pallas_call(
        plan_kernel,
        out_shape=(
            jax.ShapeDtypeStruct((4, NREC), jnp.int32),
            jax.ShapeDtypeStruct((NREC, FX), jnp.float32),
            jax.ShapeDtypeStruct((STEPS, FX), jnp.float32),
        ),
        in_specs=[VMEM] * 3,
        out_specs=(VMEM,) * 3,
        compiler_params=PARAMS,
    )(stations, sources, pulses)


def stretch(has_low, has_high, reach_out):
    first = CUR_RIM - jnp.where(has_low, reach_out, 0)
    last = CUR_RIM + PLANES + jnp.where(has_high, reach_out, 0)
    return first, last


def wave_kernel(
    plan,
    pick_ref,
    pulses_ref,
    cur_ref,
    prev_ref,
    low_0,
    high_0,
    adjoint_ref,
    speeds_ref,
    widen_ref,
    tall_ref,
    short_ref,
    narrow_ref,
    row_band_ref,
    column_band_ref,
    final_out,
    terms_ref,
    copied,
    field_a,
    field_b,
    factor,
    coarse,
    speed,
    total,
    rows_ref,
):
    slab, has_low, has_high = slab_place()
    bands = (row_band_ref, column_band_ref)
    for field in (field_a, field_b):
        clear_rows(field, 0, EXT)
        clear_beyond(field, has_low, has_high)

    for plane in range(PLANES):
        value = cur_ref[plane]
        field_a[CUR_RIM + plane, INNER, :] = value
        field_b[CUR_RIM + plane, INNER, :] = 2.0 * value - prev_ref[plane]

    def load_rim(parts, at_cur, at_prev):
        def rim(plane):
            for ref, begin, end in zip(parts, PARTS[:-1], PARTS[1:]):
                if begin <= plane < end:
                    return ref[plane - begin].astype(jnp.float32)

        for plane in range(CUR_RIM):
            field_a[at_cur + plane, INNER, :] = rim(PREV_RIM + plane)
        for plane in range(PREV_RIM):
            field_b[at_prev + plane, INNER, :] = 2.0 * field_a[
                at_prev + plane, INNER, :
            ] - rim(plane)

    @pl.when(has_low)
    def _():
        load_rim((low_0,), 0, REACH)

    @pl.when(has_high)
    def _():
        load_rim((high_0,), CUR_RIM + PLANES, CUR_RIM + PLANES)

    def widen_block(slab, at):
        block = speeds_ref[pl.ds(slab * SHOTS, SHOTS)].reshape(SHOTS * 16, 128)
        wide = jnp.dot(block, widen_ref[...], preferred_element_type=jnp.float32)
        for k in range(SHOTS):
            piece = wide[16 * k : 16 * (k + 1)]
            both = jnp.concatenate([piece[:, :128], piece[:, 128:]], axis=0)
            high, low = halves(both)
            stacked = jnp.concatenate([high, low], axis=0)
            coarse[at + k] = jnp.dot(
                tall_ref[...], stacked, preferred_element_type=jnp.float32
            )

    widen_block(slab, SHOTS)

    @pl.when(has_low)
    def _():
        widen_block(slab - 1, 0)

    @pl.when(jnp.logical_not(has_low))
    def _():
        coarse[SHOTS - 1] = coarse[SHOTS]

    @pl.when(has_high)
    def _():
        widen_block(slab + 1, 2 * SHOTS)

    @pl.when(jnp.logical_not(has_high))
    def _():
        coarse[2 * SHOTS] = coarse[2 * SHOTS - 1]

    def refine(k):
        here = 0.75 * coarse[k]
        for plane, there in ((2 * k, coarse[k - 1]), (2 * k + 1, coarse[k + 1])):
            value = here + 0.25 * there
            speed[plane] = value
            factor[plane] = (courant * value) * (courant * value)

    for k in range(CUR_RIM // 2, (CUR_RIM + PLANES) // 2):
        refine(k)
    over_rims(has_low, has_high, PREV_RIM, 2, refine)

    source_plane, source_row = plan[1, 0], plan[2, 0]
    lane_row = lax.broadcasted_iota(jnp.int32, (1, FX), 1)

    def inject(field, step, first, last):
        inside = (source_plane >= first) & (source_plane < last)
        plane = jnp.clip(source_plane, first, last - 1)
        place = (plane, pl.ds(source_row, 1), slice(None))
        field[place] = field[place] + jnp.where(
            inside & (lane_row == plan[3, 0]), pulses_ref[step : step + 1, :], 0.0
        )

    def collect(field, step, k):
        rows_ref[step, pl.ds(k, 1), :] = field.reshape(EXT * ROWS, FX)[pl.ds(plan[0, k], 1), :]

    stores = []
    for step in range(STEPS):
        now, out = (field_a, field_b) if step % 2 == 0 else (field_b, field_a)
        reach_out = CUR_RIM - REACH * (step + 1)

        def advance(plane, rows, centre, lap):
            here = (plane, slice(rows.start + PAD, rows.stop + PAD), slice(None))
            carried = out[here] if step == 0 else 2.0 * centre - out[here]
            out[here] = carried + factor[plane, rows, :] * lap

        def rim_planes(chunk):
            def use(k, rows, centre, lap):
                advance(chunk * CHUNK + k, rows, centre, lap)

            laplace(now, chunk * CHUNK, bands, use)

        def own_planes(chunk):
            begin = chunk * CHUNK

            def use(k, rows, centre, lap):
                term = adjoint_ref[step, begin + k, rows, :].astype(jnp.float32) * lap
                if step > 0:
                    term = total[begin + k, rows, :] + term
                total[begin + k, rows, :] = term
                advance(CUR_RIM + begin + k, rows, centre, lap)

            laplace(now, CUR_RIM + begin, bands, use)
            share = NREC * CHUNK // PLANES if step > 0 else 0
            for k in range(share):
                collect(now, step - 1, chunk * share + k)

        first, last = stretch(has_low, has_high, reach_out)
        for chunk in range(PLANES // CHUNK):
            own_planes(chunk)
            if reach_out == 0:
                begin = CUR_RIM + chunk * CHUNK
                inject(out, step, begin, begin + CHUNK)
                stores.append(
                    pltpu.make_async_copy(
                        out.at[pl.ds(begin, CHUNK), pl.ds(PAD, FY), :],
                        final_out.at[pl.ds(chunk * CHUNK, CHUNK)],
                        copied.at[chunk],
                    )
                )
                stores[-1].start()
        if reach_out > 0:
            over_rims(has_low, has_high, reach_out, CHUNK, rim_planes)
            inject(out, step, first, last)

    for k in range(NREC):
        collect(field_a, STEPS - 1, k)
    record = jnp.concatenate(
        [
            jnp.sum((rows_ref[step] * pick_ref[...]).T, axis=0, keepdims=True)
            for step in range(STEPS)
        ]
        + [jnp.zeros((16 - STEPS, FX), jnp.float32)],
        axis=0,
    ).astype(jnp.bfloat16)

    for plane in range(PLANES):
        total[plane] = (2.0 * courant * courant) * speed[CUR_RIM + plane] * total[plane]

    shrunk = []
    for k in range(-1, SHOTS + 1):
        value = 0.0
        for plane, weight in ((2 * k - 1, 0.25), (2 * k, 0.75), (2 * k + 1, 0.75), (2 * k + 2, 0.25)):
            if 0 <= plane < PLANES:
                value = value + weight * total[plane]
        high, low = halves(value)
        stacked = jnp.concatenate([high, low], axis=0)
        shrunk.append(jnp.dot(short_ref[...], stacked, preferred_element_type=jnp.float32))
    sides = [jnp.concatenate([z[:16], z[16:]], axis=1) for z in shrunk]
    high, low = halves(jnp.concatenate(sides, axis=0))
    narrow = narrow_ref[...]
    out = jnp.dot(high, narrow, preferred_element_type=jnp.float32) + jnp.dot(
        low, narrow, preferred_element_type=jnp.float32
    )
    below = out[:16]
    above = out[16 * (SHOTS + 1) :]

    def no_term(position, _):
        terms_ref[position, :16, :] = jnp.zeros((16, 128), jnp.bfloat16)
        terms_ref[position, 16:, :] = record
        return 0

    lax.fori_loop(0, terms_ref.shape[0], no_term, 0, unroll=8)
    for k in range(SHOTS):
        piece = out[16 * (k + 1) : 16 * (k + 2)]
        if k == 0:
            piece = piece + jnp.where(has_low, 0.0, below)
        if k == SHOTS - 1:
            piece = piece + jnp.where(has_high, 0.0, above)
        terms_ref[slab * SHOTS + k, :16, :] = piece.astype(jnp.bfloat16)

    @pl.when(has_low)
    def _():
        terms_ref[slab * SHOTS - 1, :16, :] = below.astype(jnp.bfloat16)

    @pl.when(has_high)
    def _():
        terms_ref[slab * SHOTS + SHOTS, :16, :] = above.astype(jnp.bfloat16)

    for store in stores:
        store.wait()


def wave(*args):
    devices = lax.axis_size("slab")
    return pl.pallas_call(
        wave_kernel,
        out_shape=(
            jax.ShapeDtypeStruct((PLANES, FY, FX), jnp.float32),
            jax.ShapeDtypeStruct((devices, 32, 128), jnp.bfloat16),
        ),
        in_specs=[pl.BlockSpec(memory_space=pltpu.SMEM)] + [VMEM] * 14,
        out_specs=(ANY, VMEM),
        scratch_shapes=[
            pltpu.SemaphoreType.DMA((PLANES // CHUNK,)),
            pltpu.VMEM((EXT, ROWS, FX), jnp.float32),
            pltpu.VMEM((EXT, ROWS, FX), jnp.float32),
            pltpu.VMEM((EXT, FY, FX), jnp.float32),
            pltpu.VMEM((3 * SHOTS, FY, FX), jnp.float32),
            pltpu.VMEM((EXT, FY, FX), jnp.float32),
            pltpu.VMEM((PLANES, FY, FX), jnp.float32),
            pltpu.VMEM((STEPS, NREC, FX), jnp.float32),
        ],
        compiler_params=PARAMS,
    )(*args)


def finish_kernel(terms_ref, gradient_ref, traces_ref):
    devices = terms_ref.shape[0]
    term = terms_ref[0, :16, :].astype(jnp.float32)
    for position in range(1, devices):
        term = term + terms_ref[position, :16, :].astype(jnp.float32)
    for j in range(16):
        gradient_ref[:, 128 * j : 128 * (j + 1)] = term[j : j + 1, :]
    for shot in range(SHOTS):
        record = terms_ref[shot, 16:, :].astype(jnp.float32)
        for position in range(shot + SHOTS, devices, SHOTS):
            record = record + terms_ref[position, 16:, :].astype(jnp.float32)
        traces_ref[shot] = record[:STEPS]


def finish(terms):
    return pl.pallas_call(
        finish_kernel,
        out_shape=(
            jax.ShapeDtypeStruct((1, CELLS), jnp.float32),
            jax.ShapeDtypeStruct((SHOTS, STEPS, NREC), jnp.float32),
        ),
        in_specs=[VMEM],
        out_specs=(VMEM, VMEM),
        compiler_params=PARAMS,
    )(terms)


def shift(value, steps):
    count = lax.axis_size("slab")
    begin, end = max(0, -steps), min(count, count - steps)
    return lax.ppermute(value, "slab", [(source, source + steps) for source in range(begin, end)])


def across_chips(value, boundaries):
    count = lax.axis_size("slab")
    pairs = [(i, i + 1) for i in range(1, count - 1, 2) if boundaries or (i + 1) % SHOTS > 0]
    return lax.ppermute(value, "slab", pairs + [(b, a) for a, b in pairs])


def past_boundary(value):
    pairs = []
    for first in range(SHOTS, lax.axis_size("slab"), SHOTS):
        pairs += [(first + 1, first - 1), (first - 2, first)]
    return lax.ppermute(value, "slab", pairs)


def partner(value, mask):
    count = lax.axis_size("slab")
    return lax.ppermute(value, "slab", [(source, source ^ mask) for source in range(count)])


def body(
    latent, conv1_weight, conv2_weight, head, p_prev, p_cur, adjoint, wavelet, sources, receivers
):
    position = lax.axis_index("slab")
    devices = lax.axis_size("slab")
    slabs = devices // SHOTS
    shot = position % SHOTS
    slab = position // SHOTS
    has_low = slab > 0
    has_high = slab < slabs - 1

    def exchange(to_low, to_high):
        if slabs == 2:
            got = partner(to_low if to_low is to_high else jnp.where(has_low, to_low, to_high), SHOTS)
            return got, got
        return shift(to_high, SHOTS), shift(to_low, -SHOTS)

    latent = latent.reshape(CH, CELLS)
    latent_far, latent_near = across_chips(latent, True), partner(latent, 1)
    latent_extra = past_boundary(latent)
    current = p_cur[0]
    previous = p_prev[0]
    to_low = jnp.concatenate([previous[:PREV_RIM], current], axis=0).astype(jnp.bfloat16)
    to_high = jnp.concatenate([previous[PLANES - PREV_RIM :], current], axis=0).astype(jnp.bfloat16)
    to_low = [to_low[begin:end] for begin, end in zip(PARTS[:-1], PARTS[1:])]
    to_high = [to_high[begin:end] for begin, end in zip(PARTS[:-1], PARTS[1:])]
    to_low, to_high, _ = lax.optimization_barrier(
        (to_low[0], to_high[0], (latent_far, latent_near, latent_extra))
    )
    low_0, high_0 = exchange(to_low, to_high)

    hidden, beyond = first_conv(latent_near, latent, latent_far, latent_extra, conv1_weight)
    hidden_far, hidden_near = across_chips(hidden, False), partner(hidden, 1)
    velocity = second_conv(hidden_near, hidden, hidden_far, beyond, conv2_weight, head[None])
    speeds = lax.all_to_all(
        jnp.broadcast_to(velocity[None], (devices,) + velocity.shape), "slab", 0, 0
    )

    adjoint = adjoint[:, 0]
    plan, pick, pulses = plan_wave(
        jnp.transpose(receivers, (1, 0, 2)), sources.T, wavelet.T
    )
    final, terms = wave(
        plan,
        pick,
        pulses,
        current,
        previous,
        low_0,
        high_0,
        adjoint,
        speeds,
        *plane_matrices(),
        row_band(),
        column_band(),
    )

    gradient, traces = finish(lax.all_to_all(terms, "slab", 0, 0))
    return (final[None], traces, gradient)


def solution(mesh):
    in_specs = (
        P(None, ("groups", "slab"), None),
        P(),
        P(),
        P(),
        P(("groups", "slab"), None, None, None),
        P(("groups", "slab"), None, None, None),
        P(None, ("groups", "slab"), None, None, None),
        P("groups", None),
        P("groups", None),
        P("groups", None, None),
    )
    out_specs = (
        P(("groups", "slab"), None, None, None),
        P("groups", None, None),
        P(("groups", "slab"), None),
    )
    return jax.shard_map(body, mesh=mesh, in_specs=in_specs, out_specs=out_specs, check_vma=False)
```

```python
import functools

import jax
import jax.numpy as jnp
import numpy as np
from jax import lax
from jax.experimental import pallas as pl
from jax.experimental.pallas import tpu as pltpu
from jax.sharding import PartitionSpec as P

CH = 64
CY = 32
CX = 64
FY = 64
FX = 128
CELLS = CY * CX
SHOTS = 8
STEPS = 4
NREC = 128
PLANES = 16
REACH = 4
CUR_RIM = REACH * STEPS
PREV_RIM = CUR_RIM - REACH
RIM_PLANES = CUR_RIM + PREV_RIM
PARTS = (0, RIM_PLANES)
EXT = PLANES + 2 * CUR_RIM
PAD = 8
ROWS = FY + 2 * PAD
CHUNK = 4

stencil_weights = (-205.0 / 72.0, 8.0 / 5.0, -1.0 / 5.0, 8.0 / 315.0, -1.0 / 560.0)
lowest_speed = 1.5
speed_range = 3.0
courant = 0.088
leak_slope = 0.2

VMEM = pl.BlockSpec(memory_space=pltpu.VMEM)
ANY = pl.BlockSpec(memory_space=pl.ANY)
PARAMS = pltpu.CompilerParams(vmem_limit_bytes=24 * 1024 * 1024)


def doubling_matrix(length):
    matrix = np.zeros((2 * length, length), np.float32)
    for k in range(length):
        matrix[2 * k, k] += 0.75
        matrix[2 * k, max(k - 1, 0)] += 0.25
        matrix[2 * k + 1, k] += 0.75
        matrix[2 * k + 1, min(k + 1, length - 1)] += 0.25
    return matrix


def plane_matrices():
    across = doubling_matrix(CX)
    down = doubling_matrix(CY)
    widen = np.zeros((128, 256), np.float32)
    widen[:64, :128] = across.T
    widen[64:, 128:] = across.T
    tall = np.concatenate([down[:, 0::2], down[:, 1::2]], axis=1)
    tall_twice = np.concatenate([tall, tall], axis=1)
    short_twice = np.concatenate([tall.T, tall.T], axis=1)
    narrow = widen.T
    return tuple(jnp.asarray(m, jnp.bfloat16) for m in (widen, tall_twice, short_twice, narrow))


def halves(value):
    high = value.astype(jnp.bfloat16)
    low = (value - high.astype(jnp.float32)).astype(jnp.bfloat16)
    return high, low


def leaky(value):
    return jnp.where(value > 0, value, leak_slope * value)


def at_boundary():
    place = lax.axis_index("slab")
    rank = place % SHOTS
    last = lax.axis_size("slab") - 1
    return ((rank == 0) & (place > 0)) | ((rank == SHOTS - 1) & (place < last))


def conv(near, mid, far, weight_ref, fields, packed):
    odd = lax.axis_index("slab") % 2
    depths = (2 - 2 * odd, 1, 2 * odd)
    column = lax.broadcasted_iota(jnp.int32, (CH, CELLS), 1) % CX
    for part, plane in enumerate((near, mid, far)):
        wide = plane.astype(jnp.float32)
        left = jnp.where(column == 0, 0.0, pltpu.roll(wide, 1, 1)).astype(jnp.bfloat16)
        right = jnp.where(column == CX - 1, 0.0, pltpu.roll(wide, CELLS - 1, 1)).astype(jnp.bfloat16)
        for place, piece in enumerate((left, plane, right)):
            begin = (3 * part + place) * CH
            fields[begin : begin + CH, :] = piece
    for part, depth in enumerate(depths):
        for row in range(3):
            for place in range(3):
                begin = (3 * part + place) * CH
                packed[row * CH : (row + 1) * CH, begin : begin + CH] = weight_ref[
                    9 * depth + 3 * row + place
                ]
    products = jnp.dot(packed[...], fields[...], preferred_element_type=jnp.float32)
    cell = lax.broadcasted_iota(jnp.int32, (CH, CELLS), 1)
    above = jnp.where(cell < CX, 0.0, pltpu.roll(products[:CH], CX, 1))
    below = jnp.where(cell >= CELLS - CX, 0.0, pltpu.roll(products[2 * CH :], CELLS - CX, 1))
    return products[CH : 2 * CH] + above + below


def to_column(row):
    count = row.shape[1]
    here = lax.broadcasted_iota(jnp.int32, (count, count), 0)
    there = lax.broadcasted_iota(jnp.int32, (count, count), 1)
    return jnp.sum(jnp.where(here == there, row, 0), axis=1, keepdims=True)


def first_kernel(near_ref, mid_ref, far_ref, weight_ref, out_ref, fields, packed):
    hidden = leaky(conv(near_ref[...], mid_ref[...], far_ref[...], weight_ref, fields, packed))
    out_ref[...] = hidden.astype(jnp.bfloat16)


def beyond_kernel(mid_ref, far_ref, extra_ref, weight_ref, out_ref, fields, packed):
    @pl.when(at_boundary())
    def _():
        hidden = leaky(
            conv(mid_ref[...], far_ref[...], extra_ref[...], weight_ref, fields, packed)
        )
        out_ref[...] = hidden.astype(jnp.bfloat16)


def second_kernel(
    near_ref, mid_ref, far_ref, beyond_ref, weight_ref, head_ref, out_ref, fields, packed
):
    far = jnp.where(at_boundary(), beyond_ref[...], far_ref[...])
    second = leaky(conv(near_ref[...], mid_ref[...], far, weight_ref, fields, packed))
    head = to_column(head_ref[...].astype(jnp.float32))
    logits = jnp.sum(second * head, axis=0, keepdims=True)
    speed = lowest_speed + speed_range * jax.nn.sigmoid(logits)
    for j in range(16):
        out_ref[j : j + 1, :] = speed[:, 128 * j : 128 * (j + 1)].astype(jnp.bfloat16)


CONV_SCRATCH = [
    pltpu.VMEM((9 * CH, CELLS), jnp.bfloat16),
    pltpu.VMEM((3 * CH, 9 * CH), jnp.bfloat16),
]


def first_conv(kernel, *args):
    return pl.pallas_call(
        kernel,
        out_shape=jax.ShapeDtypeStruct((CH, CELLS), jnp.bfloat16),
        in_specs=[VMEM] * 4,
        out_specs=VMEM,
        scratch_shapes=CONV_SCRATCH,
        compiler_params=PARAMS,
    )(*args)


def second_conv(near, mid, far, beyond, weight, head):
    return pl.pallas_call(
        second_kernel,
        out_shape=jax.ShapeDtypeStruct((16, 128), jnp.bfloat16),
        in_specs=[VMEM] * 6,
        out_specs=VMEM,
        scratch_shapes=CONV_SCRATCH,
        compiler_params=PARAMS,
    )(near, mid, far, beyond, weight, head)


def band_matrix(length, diagonal):
    band = np.zeros((length, length), np.float64)
    for reach, weight in enumerate(stencil_weights):
        for at in range(length):
            if reach == 0:
                band[at, at] = diagonal
            elif at + reach < length:
                band[at, at + reach] = band[at + reach, at] = weight
    high = band.astype(jnp.bfloat16)
    return high, (band - high.astype(np.float64)).astype(jnp.bfloat16)


def row_band():
    high, low = band_matrix(FX, 3.0 * stencil_weights[0])
    return jnp.asarray(np.block([[high, low], [high, np.zeros_like(low)]]))


def column_band():
    high, low = band_matrix(FY, 0.0)
    return jnp.asarray(np.concatenate([high, high, low], axis=1))


INNER = slice(PAD, PAD + FY)


def laplace(field, first, bands, use):
    planes = field[pl.ds(first, CHUNK), INNER, :].reshape(CHUNK * FY, FX)
    high, low = halves(planes)
    across = jnp.dot(
        jnp.concatenate([high, low], axis=1), bands[0][...], preferred_element_type=jnp.float32
    )

    def abreast(value):
        return jnp.concatenate([value[k * FY : (k + 1) * FY] for k in range(CHUNK)], axis=1)

    high, low = abreast(high), abreast(low)
    down = jnp.dot(
        bands[1][...],
        jnp.concatenate([high, low, high], axis=0),
        preferred_element_type=jnp.float32,
    )
    for row in range(0, FY, 8):
        column = [
            field[first + k - REACH, PAD + row : PAD + row + 8, :]
            for k in range(CHUNK + 2 * REACH)
        ]
        for k in range(CHUNK):
            begin = k * FY + row
            total = across[begin : begin + 8, :FX] + across[begin : begin + 8, FX:]
            total = total + down[row : row + 8, k * FX : (k + 1) * FX]
            for reach in range(1, REACH + 1):
                near = column[k + REACH - reach] + column[k + REACH + reach]
                total = total + stencil_weights[reach] * near
            use(k, slice(row, row + 8), column[k + REACH], total)


def slab_place():
    slab = lax.axis_index("slab") // SHOTS
    slabs = lax.axis_size("slab") // SHOTS
    return slab, slab > 0, slab < slabs - 1


def over_rims(has_low, has_high, planes, size, use):
    count = planes // size
    below, above = CUR_RIM // size - count, (CUR_RIM + PLANES) // size
    if lax.axis_size("slab") == 2 * SHOTS:
        for k in range(count):
            use(jnp.where(has_low, below, above) + k)
        return
    for inside, begin in ((has_low, below), (has_high, above)):

        @pl.when(inside)
        def _():
            for k in range(count):
                use(begin + k)


def clear_rows(field, first, last):
    def one(plane, _):
        field[plane, :PAD, :] = jnp.zeros((PAD, FX), jnp.float32)
        field[plane, PAD + FY :, :] = jnp.zeros((PAD, FX), jnp.float32)
        return 0

    lax.fori_loop(first, last, one, 0, unroll=8)


def clear_beyond(field, has_low, has_high):
    for inside, begin in ((has_low, CUR_RIM - REACH), (has_high, CUR_RIM + PLANES)):

        @pl.when(jnp.logical_not(inside))
        def _():
            for plane in range(begin, begin + REACH):
                field[plane, INNER, :] = jnp.zeros((FY, FX), jnp.float32)


def plan_kernel(stations_ref, sources_ref, pulses_ref, plan_out, pick_out, pulses_out):
    slab, _, _ = slab_place()
    shot = lax.axis_index("slab") % SHOTS
    depth = stations_ref[0, pl.ds(shot, 1), :] - slab * PLANES
    inside = (depth >= 0) & (depth < PLANES)
    column = jnp.where(inside, stations_ref[2, pl.ds(shot, 1), :], -1)
    lane = lax.broadcasted_iota(jnp.int32, (NREC, FX), 1)
    pick_out[...] = jnp.where(to_column(column) == lane, 1.0, 0.0)
    plan_out[:1, :] = (
        (jnp.clip(depth, 0, PLANES - 1) + CUR_RIM) * ROWS + PAD + stations_ref[1, pl.ds(shot, 1), :]
    )
    mine = lax.broadcasted_iota(jnp.int32, (1, SHOTS), 1) == shot
    source = jnp.sum(jnp.where(mine, sources_ref[...], 0), axis=1, keepdims=True)
    plan_out[1:2, :] = jnp.broadcast_to(source[:1] - slab * PLANES + CUR_RIM, (1, FX))
    plan_out[2:3, :] = jnp.broadcast_to(source[1:2] + PAD, (1, FX))
    plan_out[3:4, :] = jnp.broadcast_to(source[2:], (1, FX))
    pulse = jnp.sum(jnp.where(mine, pulses_ref[...], 0.0), axis=1, keepdims=True)
    pulses_out[...] = jnp.broadcast_to(pulse, (STEPS, FX))


def plan_wave(stations, sources, pulses):
    return pl.pallas_call(
        plan_kernel,
        out_shape=(
            jax.ShapeDtypeStruct((4, NREC), jnp.int32),
            jax.ShapeDtypeStruct((NREC, FX), jnp.float32),
            jax.ShapeDtypeStruct((STEPS, FX), jnp.float32),
        ),
        in_specs=[VMEM] * 3,
        out_specs=(VMEM,) * 3,
        compiler_params=PARAMS,
    )(stations, sources, pulses)


def stretch(has_low, has_high, reach_out):
    first = CUR_RIM - jnp.where(has_low, reach_out, 0)
    last = CUR_RIM + PLANES + jnp.where(has_high, reach_out, 0)
    return first, last


def wave_kernel(
    plan,
    pick_ref,
    pulses_ref,
    cur_ref,
    prev_ref,
    low_0,
    high_0,
    adjoint_ref,
    speeds_ref,
    widen_ref,
    tall_ref,
    short_ref,
    narrow_ref,
    row_band_ref,
    column_band_ref,
    final_out,
    terms_ref,
    copied,
    field_a,
    field_b,
    factor,
    coarse,
    speed,
    total,
    rows_ref,
):
    slab, has_low, has_high = slab_place()
    bands = (row_band_ref, column_band_ref)
    for field in (field_a, field_b):
        clear_rows(field, 0, EXT)
        clear_beyond(field, has_low, has_high)

    for plane in range(PLANES):
        value = cur_ref[plane]
        field_a[CUR_RIM + plane, INNER, :] = value
        field_b[CUR_RIM + plane, INNER, :] = 2.0 * value - prev_ref[plane]

    def load_rim(parts, at_cur, at_prev):
        def rim(plane):
            for ref, begin, end in zip(parts, PARTS[:-1], PARTS[1:]):
                if begin <= plane < end:
                    return ref[plane - begin].astype(jnp.float32)

        for plane in range(CUR_RIM):
            field_a[at_cur + plane, INNER, :] = rim(PREV_RIM + plane)
        for plane in range(PREV_RIM):
            field_b[at_prev + plane, INNER, :] = 2.0 * field_a[
                at_prev + plane, INNER, :
            ] - rim(plane)

    @pl.when(has_low)
    def _():
        load_rim((low_0,), 0, REACH)

    @pl.when(has_high)
    def _():
        load_rim((high_0,), CUR_RIM + PLANES, CUR_RIM + PLANES)

    def widen_block(slab, at):
        block = speeds_ref[pl.ds(slab * SHOTS, SHOTS)].reshape(SHOTS * 16, 128)
        wide = jnp.dot(block, widen_ref[...], preferred_element_type=jnp.float32)
        for k in range(SHOTS):
            piece = wide[16 * k : 16 * (k + 1)]
            both = jnp.concatenate([piece[:, :128], piece[:, 128:]], axis=0)
            high, low = halves(both)
            stacked = jnp.concatenate([high, low], axis=0)
            coarse[at + k] = jnp.dot(
                tall_ref[...], stacked, preferred_element_type=jnp.float32
            )

    widen_block(slab, SHOTS)

    @pl.when(has_low)
    def _():
        widen_block(slab - 1, 0)

    @pl.when(jnp.logical_not(has_low))
    def _():
        coarse[SHOTS - 1] = coarse[SHOTS]

    @pl.when(has_high)
    def _():
        widen_block(slab + 1, 2 * SHOTS)

    @pl.when(jnp.logical_not(has_high))
    def _():
        coarse[2 * SHOTS] = coarse[2 * SHOTS - 1]

    def refine(k):
        here = 0.75 * coarse[k]
        for plane, there in ((2 * k, coarse[k - 1]), (2 * k + 1, coarse[k + 1])):
            value = here + 0.25 * there
            speed[plane] = value
            factor[plane] = (courant * value) * (courant * value)

    for k in range(CUR_RIM // 2, (CUR_RIM + PLANES) // 2):
        refine(k)
    over_rims(has_low, has_high, PREV_RIM, 2, refine)

    source_plane, source_row = plan[1, 0], plan[2, 0]
    lane_row = lax.broadcasted_iota(jnp.int32, (1, FX), 1)

    def inject(field, step, first, last):
        inside = (source_plane >= first) & (source_plane < last)
        plane = jnp.clip(source_plane, first, last - 1)
        place = (plane, pl.ds(source_row, 1), slice(None))
        field[place] = field[place] + jnp.where(
            inside & (lane_row == plan[3, 0]), pulses_ref[step : step + 1, :], 0.0
        )

    def collect(field, step, k):
        rows_ref[step, pl.ds(k, 1), :] = field.reshape(EXT * ROWS, FX)[pl.ds(plan[0, k], 1), :]

    stores = []
    for step in range(STEPS):
        now, out = (field_a, field_b) if step % 2 == 0 else (field_b, field_a)
        reach_out = CUR_RIM - REACH * (step + 1)

        def advance(plane, rows, centre, lap):
            here = (plane, slice(rows.start + PAD, rows.stop + PAD), slice(None))
            carried = out[here] if step == 0 else 2.0 * centre - out[here]
            out[here] = carried + factor[plane, rows, :] * lap

        def rim_planes(chunk):
            def use(k, rows, centre, lap):
                advance(chunk * CHUNK + k, rows, centre, lap)

            laplace(now, chunk * CHUNK, bands, use)

        def own_planes(chunk):
            begin = chunk * CHUNK

            def use(k, rows, centre, lap):
                term = adjoint_ref[step, begin + k, rows, :].astype(jnp.float32) * lap
                if step > 0:
                    term = total[begin + k, rows, :] + term
                total[begin + k, rows, :] = term
                advance(CUR_RIM + begin + k, rows, centre, lap)

            laplace(now, CUR_RIM + begin, bands, use)
            share = NREC * CHUNK // PLANES if step > 0 else 0
            for k in range(share):
                collect(now, step - 1, chunk * share + k)

        first, last = stretch(has_low, has_high, reach_out)
        for chunk in range(PLANES // CHUNK):
            own_planes(chunk)
            if reach_out == 0:
                begin = CUR_RIM + chunk * CHUNK
                inject(out, step, begin, begin + CHUNK)
                stores.append(
                    pltpu.make_async_copy(
                        out.at[pl.ds(begin, CHUNK), pl.ds(PAD, FY), :],
                        final_out.at[pl.ds(chunk * CHUNK, CHUNK)],
                        copied.at[chunk],
                    )
                )
                stores[-1].start()
        if reach_out > 0:
            over_rims(has_low, has_high, reach_out, CHUNK, rim_planes)
            inject(out, step, first, last)

    for k in range(NREC):
        collect(field_a, STEPS - 1, k)
    record = jnp.concatenate(
        [
            jnp.sum((rows_ref[step] * pick_ref[...]).T, axis=0, keepdims=True)
            for step in range(STEPS)
        ]
        + [jnp.zeros((16 - STEPS, FX), jnp.float32)],
        axis=0,
    ).astype(jnp.bfloat16)

    for plane in range(PLANES):
        total[plane] = (2.0 * courant * courant) * speed[CUR_RIM + plane] * total[plane]

    shrunk = []
    for k in range(-1, SHOTS + 1):
        value = 0.0
        for plane, weight in ((2 * k - 1, 0.25), (2 * k, 0.75), (2 * k + 1, 0.75), (2 * k + 2, 0.25)):
            if 0 <= plane < PLANES:
                value = value + weight * total[plane]
        high, low = halves(value)
        stacked = jnp.concatenate([high, low], axis=0)
        shrunk.append(jnp.dot(short_ref[...], stacked, preferred_element_type=jnp.float32))
    sides = [jnp.concatenate([z[:16], z[16:]], axis=1) for z in shrunk]
    high, low = halves(jnp.concatenate(sides, axis=0))
    narrow = narrow_ref[...]
    out = jnp.dot(high, narrow, preferred_element_type=jnp.float32) + jnp.dot(
        low, narrow, preferred_element_type=jnp.float32
    )
    below = out[:16]
    above = out[16 * (SHOTS + 1) :]

    def no_term(position, _):
        terms_ref[position, :16, :] = jnp.zeros((16, 128), jnp.bfloat16)
        terms_ref[position, 16:, :] = record
        return 0

    lax.fori_loop(0, terms_ref.shape[0], no_term, 0, unroll=8)
    for k in range(SHOTS):
        piece = out[16 * (k + 1) : 16 * (k + 2)]
        if k == 0:
            piece = piece + jnp.where(has_low, 0.0, below)
        if k == SHOTS - 1:
            piece = piece + jnp.where(has_high, 0.0, above)
        terms_ref[slab * SHOTS + k, :16, :] = piece.astype(jnp.bfloat16)

    @pl.when(has_low)
    def _():
        terms_ref[slab * SHOTS - 1, :16, :] = below.astype(jnp.bfloat16)

    @pl.when(has_high)
    def _():
        terms_ref[slab * SHOTS + SHOTS, :16, :] = above.astype(jnp.bfloat16)

    for store in stores:
        store.wait()


def wave(*args):
    devices = lax.axis_size("slab")
    return pl.pallas_call(
        wave_kernel,
        out_shape=(
            jax.ShapeDtypeStruct((PLANES, FY, FX), jnp.float32),
            jax.ShapeDtypeStruct((devices, 32, 128), jnp.bfloat16),
        ),
        in_specs=[pl.BlockSpec(memory_space=pltpu.SMEM)] + [VMEM] * 14,
        out_specs=(ANY, VMEM),
        scratch_shapes=[
            pltpu.SemaphoreType.DMA((PLANES // CHUNK,)),
            pltpu.VMEM((EXT, ROWS, FX), jnp.float32),
            pltpu.VMEM((EXT, ROWS, FX), jnp.float32),
            pltpu.VMEM((EXT, FY, FX), jnp.float32),
            pltpu.VMEM((3 * SHOTS, FY, FX), jnp.float32),
            pltpu.VMEM((EXT, FY, FX), jnp.float32),
            pltpu.VMEM((PLANES, FY, FX), jnp.float32),
            pltpu.VMEM((STEPS, NREC, FX), jnp.float32),
        ],
        compiler_params=PARAMS,
    )(*args)


def finish_kernel(terms_ref, gradient_ref, traces_ref):
    devices = terms_ref.shape[0]
    term = terms_ref[0, :16, :].astype(jnp.float32)
    for position in range(1, devices):
        term = term + terms_ref[position, :16, :].astype(jnp.float32)
    for j in range(16):
        gradient_ref[:, 128 * j : 128 * (j + 1)] = term[j : j + 1, :]
    for shot in range(SHOTS):
        record = terms_ref[shot, 16:, :].astype(jnp.float32)
        for position in range(shot + SHOTS, devices, SHOTS):
            record = record + terms_ref[position, 16:, :].astype(jnp.float32)
        traces_ref[shot] = record[:STEPS]


def finish(terms):
    return pl.pallas_call(
        finish_kernel,
        out_shape=(
            jax.ShapeDtypeStruct((1, CELLS), jnp.float32),
            jax.ShapeDtypeStruct((SHOTS, STEPS, NREC), jnp.float32),
        ),
        in_specs=[VMEM],
        out_specs=(VMEM, VMEM),
        compiler_params=PARAMS,
    )(terms)


def shift(value, steps):
    count = lax.axis_size("slab")
    begin, end = max(0, -steps), min(count, count - steps)
    return lax.ppermute(value, "slab", [(source, source + steps) for source in range(begin, end)])


def across_chips(value, boundaries):
    count = lax.axis_size("slab")
    pairs = [(i, i + 1) for i in range(1, count - 1, 2) if boundaries or (i + 1) % SHOTS > 0]
    return lax.ppermute(value, "slab", pairs + [(b, a) for a, b in pairs])


def past_boundary(value):
    pairs = []
    for first in range(SHOTS, lax.axis_size("slab"), SHOTS):
        pairs += [(first + 1, first - 1), (first - 2, first)]
    return lax.ppermute(value, "slab", pairs)


def partner(value, mask):
    count = lax.axis_size("slab")
    return lax.ppermute(value, "slab", [(source, source ^ mask) for source in range(count)])


def body(
    latent, conv1_weight, conv2_weight, head, p_prev, p_cur, adjoint, wavelet, sources, receivers
):
    position = lax.axis_index("slab")
    devices = lax.axis_size("slab")
    slabs = devices // SHOTS
    shot = position % SHOTS
    slab = position // SHOTS
    has_low = slab > 0
    has_high = slab < slabs - 1

    def exchange(to_low, to_high):
        if slabs == 2:
            got = partner(to_low if to_low is to_high else jnp.where(has_low, to_low, to_high), SHOTS)
            return got, got
        return shift(to_high, SHOTS), shift(to_low, -SHOTS)

    latent = latent.reshape(CH, CELLS)
    latent_far, latent_near = across_chips(latent, True), partner(latent, 1)
    latent_extra = past_boundary(latent)
    current = p_cur[0]
    previous = p_prev[0]
    to_low = jnp.concatenate([previous[:PREV_RIM], current], axis=0).astype(jnp.bfloat16)
    to_high = jnp.concatenate([previous[PLANES - PREV_RIM :], current], axis=0).astype(jnp.bfloat16)
    to_low = [to_low[begin:end] for begin, end in zip(PARTS[:-1], PARTS[1:])]
    to_high = [to_high[begin:end] for begin, end in zip(PARTS[:-1], PARTS[1:])]
    to_low, to_high, _ = lax.optimization_barrier(
        (to_low[0], to_high[0], (latent_far, latent_near, latent_extra))
    )
    low_0, high_0 = exchange(to_low, to_high)

    hidden = first_conv(first_kernel, latent_near, latent, latent_far, conv1_weight)
    hidden_far, hidden_near = across_chips(hidden, False), partner(hidden, 1)
    beyond = first_conv(beyond_kernel, latent, latent_far, latent_extra, conv1_weight)
    velocity = second_conv(hidden_near, hidden, hidden_far, beyond, conv2_weight, head[None])
    speeds = lax.all_to_all(
        jnp.broadcast_to(velocity[None], (devices,) + velocity.shape), "slab", 0, 0
    )

    adjoint = adjoint[:, 0]
    plan, pick, pulses = plan_wave(
        jnp.transpose(receivers, (1, 0, 2)), sources.T, wavelet.T
    )
    final, terms = wave(
        plan,
        pick,
        pulses,
        current,
        previous,
        low_0,
        high_0,
        adjoint,
        speeds,
        *plane_matrices(),
        row_band(),
        column_band(),
    )

    gradient, traces = finish(lax.all_to_all(terms, "slab", 0, 0))
    return (final[None], traces, gradient)


def solution(mesh):
    in_specs = (
        P(None, ("groups", "slab"), None),
        P(),
        P(),
        P(),
        P(("groups", "slab"), None, None, None),
        P(("groups", "slab"), None, None, None),
        P(None, ("groups", "slab"), None, None, None),
        P("groups", None),
        P("groups", None),
        P("groups", None, None),
    )
    out_specs = (
        P(("groups", "slab"), None, None, None),
        P("groups", None, None),
        P(("groups", "slab"), None),
    )
    return jax.shard_map(body, mesh=mesh, in_specs=in_specs, out_specs=out_specs, check_vma=False)
```
